128 devices in a mesh: row: 16 (over y, x_hi, core), col: 8 (over z, x_lo).
Axes of the slice: x: 4 (x_hi: 2, x_lo: 2; x = x_hi * 2 + x_lo), y: 4, z: 4, core: 2. Of those that a mesh axis runs over, the one named last changes fastest.
Arguments:
- pair_block: bfloat16 [64, 4096, 128], P('row', 'col'), may hold values from -6 to 6
- norm_gain: float32 [128], replicated, may hold values from 0.1 to 1.9
- w_project: bfloat16 [128, 512], replicated, may hold values from -0.5 to 0.5
- w_out: bfloat16 [128, 128], replicated, may hold values from -6 to 6
- head_bias: bfloat16 [4, 4096, 4096], P(None, 'col', 'row'), may hold values from -8 to 250
Outputs:
- ending_update: bfloat16 [4096, 64, 128], P(('col', 'row'))
The draws below stay inside these ranges and needn't reach their ends.
All inputs are finite; a program needn't handle non-finite values.
Results may differ from the reference program's by a relative error of at most 0.0095.
Values may be sent and summed in bfloat16 or wider, within the bound.
No kernel may reach another device: no remote copies, remote signals or barrier semaphores. Data moves between devices by JAX's collectives and lax.ppermute only.
A program may use at most 192 MiB of HBM per device.

```python
import jax
import jax.numpy as jnp
from jax import lax

C = 128
H = 4
DH = 32
N = 4096
ROWS = 64
HD = 128


def draw_head_bias(key, part):
    key = jax.random.fold_in(key, 7)
    subkeys = jax.random.split(key, 1)
    full_shape = (H, N, N)
    values = jnp.clip(2.0 * jax.random.normal(subkeys[0], full_shape, jnp.float32), -8.0, 8.0)
    return values.astype(jnp.bfloat16)


def block_scale(rng, shape, cuts, low, top_value):
    level, own = 1.0, jax.random.fold_in(rng, 6)
    for axis_at, shards_of in cuts:
        steps = jnp.exp(jax.random.uniform(jax.random.fold_in(own, axis_at), (shards_of,), jnp.float32, low / len(cuts), top_value / len(cuts)))
        level = level * jnp.repeat(steps, shape[axis_at] // shards_of).reshape([-1 if axis == axis_at else 1 for axis in range(len(shape))])
    return level


def gaussian(stream_key, extent, deviation, most, cuts=(), dtype=jnp.bfloat16):
    drawn = deviation * jax.random.normal(stream_key, extent, jnp.float32)
    if cuts:
        drawn = drawn * block_scale(stream_key, extent, cuts, -0.22, 0.18)
    return jnp.clip(drawn, -most, most).astype(dtype)


def setup_inputs(seed: int = 0) -> dict:
    streams_of = jax.random.split(jax.random.key(seed), 6)
    return {
        "pair_block": gaussian(streams_of[0], (ROWS, N, C), 1.0, 6.0, ((0, 16), (1, 8))),
        "norm_gain": jnp.clip(1.0 + 0.18 * jax.random.normal(streams_of[1], (C,), jnp.float32), 0.1, 1.9),
        "w_project": gaussian(streams_of[2], (C, 4 * HD), C ** -0.5, 0.5),
        "w_out": gaussian(streams_of[3], (HD, C), (8 * HD ** -0.5), 6.0),
        "head_bias": draw_head_bias(jax.random.fold_in(streams_of[5], 71), 0),
    }


def layer_norm(pair_block, norm_gain):
    values = pair_block.astype(jnp.float32)
    centered = values - lax.optimization_barrier(jnp.mean(values, axis=-1, keepdims=True))
    variance = lax.optimization_barrier(jnp.mean(centered * centered, axis=-1, keepdims=True))
    return (centered * lax.rsqrt(variance + 1e-05) * norm_gain).astype(jnp.bfloat16)

def reference(pair_block, norm_gain, w_project, w_out, head_bias):
    normed = layer_norm(pair_block, norm_gain)
    projected = jnp.dot(normed.reshape(ROWS * N, C), w_project, preferred_element_type=jnp.float32)
    projected = projected.reshape(ROWS, N, 4 * HD)
    queries = (projected[..., :HD] * DH ** (-0.5)).astype(jnp.bfloat16).reshape(ROWS, N, H, DH)
    key_rows = projected[..., HD:2 * HD].astype(jnp.bfloat16).reshape(ROWS, N, H, DH)
    value_rows = projected[..., 2 * HD:3 * HD].astype(jnp.bfloat16).reshape(ROWS, N, H, DH)
    gates = jax.nn.sigmoid(projected[..., 3 * HD:])

    def one_row(row_items):
        query_row, key_row, value_row = row_items
        scores = jnp.einsum('jhd,khd->hjk', query_row.astype(jnp.float32), key_row.astype(jnp.float32))
        scores = scores + head_bias.astype(jnp.float32)
        largest = lax.optimization_barrier(jnp.max(scores, axis=-1, keepdims=True))
        exponent = jnp.exp(scores - largest)
        running_sum = lax.optimization_barrier(jnp.sum(exponent, axis=-1))
        rounded = exponent.astype(jnp.bfloat16)
        attended = jnp.einsum('hjk,khd->jhd', rounded.astype(jnp.float32), value_row.astype(jnp.float32))
        return (attended / jnp.transpose(running_sum)[:, :, None]).reshape(N, HD)
    attended = lax.map(one_row, (queries, key_rows, value_rows))
    gated = (gates * attended).astype(jnp.bfloat16)
    update = jnp.dot(gated.reshape(ROWS * N, HD), w_out, preferred_element_type=jnp.float32)
    update = update.astype(jnp.bfloat16).reshape(ROWS, N, C)
    return jnp.transpose(update, (1, 0, 2))
```

```python
import functools

import jax
import jax.numpy as jnp
from jax import lax
from jax.experimental import pallas as pl
from jax.experimental.pallas import tpu as pltpu
from jax.sharding import Mesh, PartitionSpec as P

F32, BF16 = jnp.float32, jnp.bfloat16
HEADS, WIDTH, CHANNELS = 4, 32, 128
COLS, BLOCK, ROWS = 512, 512, 4
KEYS = 4 * BLOCK
PAD = 40
LOG2E = 1.4426950408889634
ROW_AXES = ("y", "xh", "core")
COL_AXES = ("z", "xl")
CONTRACT_FIRST = (((0,), (1,)), ((), ()))


def matmul(a, b, dims=(((1,), (0,)), ((), ()))):
    return lax.dot_general(a, b, dims, preferred_element_type=F32)


def layer_norm(pair_block, norm_gain):
    values = pair_block.astype(F32)
    centered = values - jnp.mean(values, axis=-1, keepdims=True)
    variance = jnp.mean(centered * centered, axis=-1, keepdims=True)
    return (centered * lax.rsqrt(variance + 1e-05) * norm_gain).astype(BF16)


def attend_kernel(xq, xk0, xk1, xk2a, xk2b, xk3, w, *rest):
    biases, (out, lse), (bias_s, k_s, v_s, q_s, sems) = rest[:8], rest[8:10], rest[10:]
    row = pl.program_id(0)
    y, z, core = lax.axis_index("y"), lax.axis_index("z"), lax.axis_index("core")

    def bias_copies():
        copies = []
        for n, ref in enumerate(biases):
            step, other = (0, 1, 3, 2)[n // 2], n % 2
            slot = lax.rem(y + step - z + 4, 4)
            half = core if other == 0 else 1 - core
            dst = bias_s.at[slot, :, pl.ds(pl.multiple_of(half * 256, 256), 256), :]
            copies.append(pltpu.make_async_copy(ref, dst, sems.at[n]))
        return copies

    @pl.when(row == 0)
    def _():
        for copy in bias_copies():
            copy.start()
        q_s[...] = jnp.zeros_like(q_s)
        v_s[:, WIDTH:, :] = jnp.ones((HEADS, PAD - WIDTH, KEYS), BF16)

    x_q = xq[0]
    q_t = matmul(w[:, :128], x_q, CONTRACT_FIRST) * WIDTH ** (-0.5)
    q_t = q_t.astype(BF16)
    gate_t = jax.nn.sigmoid(matmul(w[:, 384:], x_q, CONTRACT_FIRST))
    for h in range(HEADS):
        q_s[h, h * WIDTH : (h + 1) * WIDTH, :] = q_t[h * WIDTH : (h + 1) * WIDTH]
    start = 0
    for x in (xk0, xk1, xk2a, xk2b, xk3):
        x_k = x[0]
        size = x_k.shape[0]
        at = slice(start, start + size)
        k_s[at, :] = matmul(x_k, w[:, 128:256]).astype(BF16)
        v_t = matmul(w[:, 256:384], x_k, CONTRACT_FIRST).astype(BF16)
        for h in range(HEADS):
            v_s[h, :WIDTH, at] = v_t[h * WIDTH : (h + 1) * WIDTH]
        start += size

    @pl.when(row == 0)
    def _():
        for copy in bias_copies():
            copy.wait()

    parts = []
    for h in range(HEADS):
        q = q_s[h]

        def scores(t):
            at = slice(t * BLOCK, (t + 1) * BLOCK)
            return matmul(k_s[at, :], q) + bias_s[t, h].astype(F32)

        s = scores(0)
        largest = total = None
        for t in range(4):
            ahead = scores(t + 1) if t < 3 else None
            top = jnp.max(s, axis=0, keepdims=True)
            fresh = top if t == 0 else jnp.maximum(largest, top)
            p = jnp.exp2((s - fresh) * LOG2E).astype(BF16)
            pv = matmul(v_s[h, :, t * BLOCK : (t + 1) * BLOCK], p)
            total = pv if t == 0 else total * jnp.exp2((largest - fresh) * LOG2E) + pv
            largest, s = fresh, ahead
        mass = total[WIDTH : WIDTH + 1]
        lse[0, h : h + 1, :] = largest + jnp.log(mass)
        parts.append(total[:WIDTH] * (1.0 / mass))
    gated = jnp.concatenate(parts, axis=0) * gate_t
    out[0] = gated.T.astype(BF16)


def attend(x_q, x_ks, w_project, biases):
    def rows(x):
        return pl.BlockSpec((1,) + x.shape[1:], lambda i: (i, 0, 0))

    count = x_q.shape[0]
    scores = count * HEADS * COLS * KEYS
    return pl.pallas_call(
        attend_kernel,
        grid=(count,),
        in_specs=[rows(x_q)]
        + [rows(x) for x in x_ks]
        + [pl.BlockSpec((CHANNELS, 512), lambda i: (0, 0))]
        + [pl.BlockSpec(memory_space=pl.ANY)] * 8,
        out_specs=[
            pl.BlockSpec((1, COLS, CHANNELS), lambda i: (i, 0, 0)),
            pl.BlockSpec((1, HEADS, COLS), lambda i: (i, 0, 0)),
        ],
        out_shape=[
            jax.ShapeDtypeStruct((count, COLS, CHANNELS), BF16),
            jax.ShapeDtypeStruct((count, HEADS, COLS), F32),
        ],
        scratch_shapes=[
            pltpu.VMEM((4, HEADS, BLOCK, COLS), BF16),
            pltpu.VMEM((KEYS, CHANNELS), BF16),
            pltpu.VMEM((HEADS, PAD, KEYS), BF16),
            pltpu.VMEM((HEADS, CHANNELS, COLS), BF16),
            pltpu.SemaphoreType.DMA((8,)),
        ],
        compiler_params=pltpu.CompilerParams(vmem_limit_bytes=56 * 2**20),
        cost_estimate=pl.CostEstimate(
            flops=scores * 512, bytes_accessed=2**24, transcendentals=scores
        ),
        name="attend",
    )(x_q, *x_ks, w_project, *biases)


def ring(step):
    return [(i, (i + step) % 4) for i in range(4)]


def shift(x, axis, step):
    return lax.ppermute(x, axis, ring(step))


def gather_ring(x, axis, cut):
    behind, ahead = shift(x, axis, 1), shift(x, axis, -1)
    half = x.shape[cut] // 2
    far_a = shift(lax.slice_in_dim(behind, 0, half, axis=cut), axis, 1)
    far_b = shift(lax.slice_in_dim(ahead, half, 2 * half, axis=cut), axis, -1)
    return x, ahead, far_a, far_b, behind


def shards(pair_block, norm_gain, w_project, w_out, head_bias):
    xh, xl = lax.axis_index("xh"), lax.axis_index("xl")
    own = layer_norm(pair_block, norm_gain)
    bias_t = jnp.transpose(head_bias, (0, 2, 1))

    x_axis = ("xh", "xl")
    beside = lax.ppermute(own, x_axis, [(0, 1), (3, 2)])
    across = lax.ppermute(own, x_axis, [(1, 2), (2, 1)])
    first_k = jnp.where(xl == xh, own, beside)
    passed = lax.ppermute(across, x_axis, [(1, 0), (2, 3)])
    second_k = jnp.where(xl == xh, passed, across)
    partner = lax.ppermute(own, x_axis, [(3, 1), (0, 2)])
    second_q = jnp.where(xl == xh, passed, partner)

    b0, b1, b2a, b2b, b3 = gather_ring(bias_t, "y", 0)
    b2 = jnp.concatenate([b2a, b2b], axis=0)
    biases = []
    for b in (b0, b1, b3, b2):
        biases += [b, lax.ppermute(b, "core", [(0, 1), (1, 0)])]

    first_ks = gather_ring(first_k, "z", 1)
    second_ks = gather_ring(second_k, "z", 1)

    out1, lse1 = attend(own, first_ks, w_project, biases)
    out2, lse2 = attend(second_q, second_ks, w_project, biases)

    def spread(x, axis):
        return lax.all_to_all(x, ROW_AXES, split_axis=axis, concat_axis=0, tiled=True)

    def flip(x):
        return x.reshape((4, 2, 8) + x.shape[1:])[:, ::-1].reshape(x.shape)

    out1, out2 = spread(out1, 1), flip(spread(out2, 1))
    lse1, lse2 = spread(lse1, 2), flip(spread(lse2, 2))
    lanes = (jnp.arange(CHANNELS)[None, :] // WIDTH == jnp.arange(HEADS)[:, None]).astype(F32)
    share = jax.nn.sigmoid(lse1 - lse2)
    share = jnp.einsum("rhj,hl->rjl", share, lanes, precision=lax.Precision.HIGHEST)
    out2 = out2.astype(F32)
    gated = (out2 + share * (out1.astype(F32) - out2)).astype(BF16)
    return jnp.einsum("ijf,fc->jic", gated, w_out, preferred_element_type=F32).astype(BF16)


def solution(mesh):
    fine = Mesh(mesh.devices.reshape(4, 2, 2, 4, 2), ROW_AXES + COL_AXES)
    in_specs = (P(ROW_AXES, COL_AXES, None), P(), P(), P(), P(None, COL_AXES, ROW_AXES))
    out_specs = P(COL_AXES + ROW_AXES, None, None)
    return jax.shard_map(
        shards, mesh=fine, in_specs=in_specs, out_specs=out_specs, check_vma=False
    )
```

```python
import jax
import jax.numpy as jnp
from jax import lax
from jax.experimental import pallas as pl
from jax.experimental.pallas import tpu as pltpu
from jax.sharding import Mesh, PartitionSpec as P

F32, BF16 = jnp.float32, jnp.bfloat16
HEADS, WIDTH, CHANNELS = 4, 32, 128
COLS, BLOCK, ROWS = 512, 512, 4
KEYS = 4 * BLOCK
SHARE = COLS // 16
PAD = 40
STEP = 2
LOG2E = 1.4426950408889634
LOW, HIGH = 1e-26, 1e30
ROW_AXES = ("y", "xh", "core")
COL_AXES = ("z", "xl")
VMEM_LIMIT = 60 * 2**20


def matmul(a, b, first=1, second=0):
    dims = (((first,), (second,)), ((), ()))
    return lax.dot_general(a, b, dims, preferred_element_type=F32)


def prepare_kernel(pair, gain, bias, normed, bias_t):
    values = pair[0].astype(F32)
    centered = values - jnp.mean(values, axis=-1, keepdims=True)
    variance = jnp.mean(centered * centered, axis=-1, keepdims=True)
    normed[0] = (centered * lax.rsqrt(variance + 1e-05) * gain[...]).astype(BF16)
    bias_t[0] = bias[0].astype(F32).T.astype(BF16)


def prepare(pair_block, norm_gain, head_bias):
    def whole(*shape):
        return pl.BlockSpec((1,) + shape, lambda i: (i, 0, 0))

    keys = head_bias.shape[2]
    return pl.pallas_call(
        prepare_kernel,
        grid=(ROWS,),
        in_specs=[
            whole(COLS, CHANNELS),
            pl.BlockSpec((1, CHANNELS), lambda i: (0, 0)),
            whole(COLS, keys),
        ],
        out_specs=[whole(COLS, CHANNELS), whole(keys, COLS)],
        out_shape=[
            jax.ShapeDtypeStruct((ROWS, COLS, CHANNELS), BF16),
            jax.ShapeDtypeStruct((HEADS, keys, COLS), BF16),
        ],
        name="prepare",
    )(pair_block, norm_gain.reshape(1, CHANNELS), head_bias)


def attend_kernel(xq, xk0, xk1, xk2a, xk2b, xk3, w, bias, out, *scratch):
    bias_s, top_s, k_s, v_s, q_s, gate_s, stat_s, sems = scratch
    step = pl.program_id(0)
    z = lax.axis_index("z")

    def bias_copies():
        copies = []
        for t in range(4):
            for c in range(2):
                src = bias.at[lax.rem(z + t, 4) * 2 + c]
                dst = bias_s.at[t, :, pl.ds(c * 256, 256), :]
                copies.append(pltpu.make_async_copy(src, dst, sems.at[t * 2 + c]))
        return copies

    @pl.when(step == 0)
    def _():
        for copy in bias_copies():
            copy.start()
        q_s[...] = jnp.zeros_like(q_s)
        stat_s[...] = jnp.zeros_like(stat_s)
        v_s[:, :, WIDTH:, :] = jnp.ones((STEP, HEADS, PAD - WIDTH, KEYS), BF16)

    def project(r):
        x_q = xq[r]
        q_t = (matmul(w[:, :128], x_q, 0, 1) * WIDTH ** (-0.5)).astype(BF16)
        gate_s[r] = jax.nn.sigmoid(matmul(w[:, 384:], x_q, 0, 1))
        for h in range(HEADS):
            at = slice(h * WIDTH, (h + 1) * WIDTH)
            q_s[r, h, at, :] = q_t[at]
        start = 0
        for x in (xk0, xk1, xk2a, xk2b, xk3):
            size = x.shape[1]
            at = slice(start, start + size)
            k_s[r, at, :] = matmul(x[r], w[:, 128:256]).astype(BF16)
            v_t = matmul(w[:, 256:384], x[r], 0, 1).astype(BF16)
            for h in range(HEADS):
                v_s[r, h, :WIDTH, at] = v_t[h * WIDTH : (h + 1) * WIDTH]
            start += size

    def finish(r, totals, shifts):
        parts, stats = [], []
        for total, shift in zip(totals, shifts):
            mass = total[WIDTH : WIDTH + 1]
            parts.append(total[:WIDTH] * (1.0 / mass))
            stats.append(shift + jnp.log(mass))
        gated = jnp.concatenate(parts, axis=0) * gate_s[r]
        at = step * STEP + r
        out[:, at] = gated.T.astype(BF16).reshape(16, SHARE, CHANNELS)
        stat = jnp.concatenate(stats, axis=0)
        high = stat.astype(BF16).astype(F32)
        middle = (stat - high).astype(BF16).astype(F32)
        low = stat - high - middle
        rows = jnp.concatenate([high, middle, low, jnp.zeros_like(low)], axis=0)
        stat_s[pl.ds(pl.multiple_of(at * 32, 32), 16), :] = rows

    for r in range(STEP):
        project(r)

    @pl.when(step == 0)
    def _():
        for copy in bias_copies():
            copy.wait()
        for h in range(HEADS):
            tops = [jnp.max(bias_s[t, h], axis=0, keepdims=True) for t in range(4)]
            top = jnp.maximum(jnp.maximum(tops[0], tops[1]), jnp.maximum(tops[2], tops[3]))
            top_s[h : h + 1, :] = top.astype(F32)

    fine = []
    for r in range(STEP):
        totals, shifts = [], []
        for h in range(HEADS):
            q, shift = q_s[r, h], top_s[h : h + 1, :]
            total = None
            for t in range(4):
                at = slice(t * BLOCK, (t + 1) * BLOCK)
                s = matmul(k_s[r, at, :], q) + bias_s[t, h].astype(F32)
                p = jnp.exp2((s - shift) * LOG2E).astype(BF16)
                pv = matmul(v_s[r, h, :, at], p)
                total = pv if t == 0 else total + pv
            totals.append(total)
            shifts.append(shift)
        finish(r, totals, shifts)
        mass = jnp.concatenate([total[WIDTH : WIDTH + 1] for total in totals], axis=0)
        inside = jnp.logical_and(mass > LOW, mass < HIGH)
        fine.append(jnp.min(inside.astype(F32)) > 0.5)

    for r in range(STEP):

        @pl.when(jnp.logical_not(fine[r]))
        def _():
            totals, shifts = [], []
            for h in range(HEADS):

                def tile(t, carry):
                    largest, total = carry
                    at = pl.ds(pl.multiple_of(t * BLOCK, BLOCK), BLOCK)
                    s = matmul(k_s[r, at, :], q_s[r, h]) + bias_s[t, h].astype(F32)
                    fresh = jnp.maximum(largest, jnp.max(s, axis=0, keepdims=True))
                    p = jnp.exp2((s - fresh) * LOG2E).astype(BF16)
                    scale = jnp.exp2((largest - fresh) * LOG2E)
                    return fresh, total * scale + matmul(v_s[r, h, :, at], p)

                begin = jnp.full((1, COLS), -jnp.inf, F32), jnp.zeros((PAD, COLS), F32)
                largest, total = lax.fori_loop(0, 4, tile, begin)
                totals.append(total)
                shifts.append(largest)
            finish(r, totals, shifts)

    @pl.when(step == pl.num_programs(0) - 1)
    def _():
        out[:, ROWS] = stat_s[...].T.astype(BF16).reshape(16, SHARE, CHANNELS)


def attend(x_q, x_ks, w_project, bias):
    def rows(x):
        return pl.BlockSpec((STEP,) + x.shape[1:], lambda i: (i, 0, 0))

    scores = ROWS * HEADS * COLS * KEYS
    message = (16, ROWS + 1, SHARE, CHANNELS)
    return pl.pallas_call(
        attend_kernel,
        grid=(ROWS // STEP,),
        in_specs=[rows(x_q)]
        + [rows(x) for x in x_ks]
        + [pl.BlockSpec((CHANNELS, 512), lambda i: (0, 0))]
        + [pl.BlockSpec(memory_space=pl.ANY)],
        out_specs=pl.BlockSpec(message, lambda i: (0, 0, 0, 0)),
        out_shape=jax.ShapeDtypeStruct(message, BF16),
        scratch_shapes=[
            pltpu.VMEM((4, HEADS, BLOCK, COLS), BF16),
            pltpu.VMEM((HEADS, COLS), F32),
            pltpu.VMEM((STEP, KEYS, CHANNELS), BF16),
            pltpu.VMEM((STEP, HEADS, PAD, KEYS), BF16),
            pltpu.VMEM((STEP, HEADS, CHANNELS, COLS), BF16),
            pltpu.VMEM((STEP, CHANNELS, COLS), F32),
            pltpu.VMEM((CHANNELS, COLS), F32),
            pltpu.SemaphoreType.DMA((8,)),
        ],
        compiler_params=pltpu.CompilerParams(vmem_limit_bytes=VMEM_LIMIT),
        cost_estimate=pl.CostEstimate(
            flops=scores * 512, bytes_accessed=2**24, transcendentals=scores
        ),
        name="attend",
    )(x_q, *x_ks, w_project, bias)


def merge_kernel(m1, m2, w, out):
    lane = lax.broadcasted_iota(jnp.int32, (CHANNELS, CHANNELS), 0)
    head = lax.broadcasted_iota(jnp.int32, (CHANNELS, CHANNELS), 1) // WIDTH
    stat1 = m1[:, ROWS].reshape(16 * SHARE, CHANNELS)
    stat2 = jnp.concatenate([m2[s ^ 2, ROWS] for s in range(16)], axis=0)
    for i in range(ROWS):
        part = lane - 32 * i
        inside = (part >= 0) & (part < 12) & (lax.rem(part, 4) == head)
        pick = inside.astype(F32).astype(BF16)
        share = jax.nn.sigmoid(matmul(stat1, pick) - matmul(stat2, pick))
        o1 = m1[:, i].reshape(16 * SHARE, CHANNELS).astype(F32)
        o2 = jnp.concatenate([m2[s ^ 2, i] for s in range(16)], axis=0).astype(F32)
        gated = (o2 + share * (o1 - o2)).astype(BF16)
        out[:, i] = matmul(gated, w[...]).astype(BF16).reshape(16, SHARE, CHANNELS)


def merge(m1, m2, w_out):
    return pl.pallas_call(
        merge_kernel,
        out_shape=jax.ShapeDtypeStruct((16, ROWS, SHARE, CHANNELS), BF16),
        compiler_params=pltpu.CompilerParams(vmem_limit_bytes=VMEM_LIMIT),
        name="merge",
    )(m1, m2, w_out)


def shift(x, axis, step):
    return lax.ppermute(x, axis, [(i, (i + step) % 4) for i in range(4)])


def gather_ring(x, axis, cut):
    behind, ahead = shift(x, axis, 1), shift(x, axis, -1)
    half = x.shape[cut] // 2
    far_a = shift(lax.slice_in_dim(behind, 0, half, axis=cut), axis, 1)
    far_b = shift(lax.slice_in_dim(ahead, half, 2 * half, axis=cut), axis, -1)
    return x, ahead, far_a, far_b, behind


def shards(pair_block, norm_gain, w_project, w_out, head_bias):
    xh, xl = lax.axis_index("xh"), lax.axis_index("xl")
    own, bias_t = prepare(pair_block, norm_gain, head_bias)

    x_axis = ("xh", "xl")
    beside = lax.ppermute(own, x_axis, [(0, 1), (3, 2)])
    across = lax.ppermute(own, x_axis, [(1, 2), (2, 1)])
    first_k = jnp.where(xl == xh, own, beside)
    passed = lax.ppermute(across, x_axis, [(1, 0), (2, 3)])
    second_k = jnp.where(xl == xh, passed, across)
    partner = lax.ppermute(own, x_axis, [(3, 1), (0, 2)])
    second_q = jnp.where(xl == xh, passed, partner)

    bias = lax.all_gather(bias_t, ("y", "core"), axis=0, tiled=False)
    first_ks = gather_ring(first_k, "z", 1)
    second_ks = gather_ring(second_k, "z", 1)

    def spread(x):
        return lax.all_to_all(x, ROW_AXES, split_axis=0, concat_axis=0, tiled=True)

    m1 = spread(attend(own, first_ks, w_project, bias))
    m2 = spread(attend(second_q, second_ks, w_project, bias))
    update = merge(m1, m2, w_out)
    return jnp.transpose(update, (2, 0, 1, 3)).reshape(SHARE, 16 * ROWS, CHANNELS)


def solution(mesh):
    fine = Mesh(mesh.devices.reshape(4, 2, 2, 4, 2), ROW_AXES + COL_AXES)
    in_specs = (P(ROW_AXES, COL_AXES, None), P(), P(), P(), P(None, COL_AXES, ROW_AXES))
    out_specs = P(COL_AXES + ROW_AXES, None, None)
    return jax.shard_map(
        shards, mesh=fine, in_specs=in_specs, out_specs=out_specs, check_vma=False
    )
```

```python
import jax
import jax.numpy as jnp
from jax import lax
from jax.experimental import pallas as pl
from jax.experimental.pallas import tpu as pltpu
from jax.sharding import Mesh, PartitionSpec as P

F32, BF16 = jnp.float32, jnp.bfloat16
HEADS, WIDTH, CHANNELS = 4, 32, 128
COLS, BLOCK, ROWS = 512, 512, 4
KEYS = 4 * BLOCK
SHARE = COLS // 16
PAD = 40
STEP = 2
LOG2E = 1.4426950408889634
LOW, HIGH = 1e-26, 1e30
ROW_AXES = ("y", "xh", "core")
COL_AXES = ("z", "xl")
VMEM_LIMIT = 60 * 2**20


def matmul(a, b, first=1, second=0):
    dims = (((first,), (second,)), ((), ()))
    return lax.dot_general(a, b, dims, preferred_element_type=F32)


def prepare_kernel(pair, gain, bias, normed, bias_t):
    values = pair[0].astype(F32)
    centered = values - jnp.mean(values, axis=-1, keepdims=True)
    variance = jnp.mean(centered * centered, axis=-1, keepdims=True)
    normed[0] = (centered * lax.rsqrt(variance + 1e-05) * gain[...]).astype(BF16)
    bias_t[0] = bias[0].astype(F32).T.astype(BF16)


def prepare(pair_block, norm_gain, head_bias):
    def whole(*shape):
        return pl.BlockSpec((1,) + shape, lambda i: (i, 0, 0))

    keys = head_bias.shape[2]
    return pl.pallas_call(
        prepare_kernel,
        grid=(ROWS,),
        in_specs=[
            whole(COLS, CHANNELS),
            pl.BlockSpec((1, CHANNELS), lambda i: (0, 0)),
            whole(COLS, keys),
        ],
        out_specs=[whole(COLS, CHANNELS), whole(keys, COLS)],
        out_shape=[
            jax.ShapeDtypeStruct((ROWS, COLS, CHANNELS), BF16),
            jax.ShapeDtypeStruct((HEADS, keys, COLS), BF16),
        ],
        name="prepare",
    )(pair_block, norm_gain.reshape(1, CHANNELS), head_bias)


def attend_kernel(xq, xk0, xk1, xk2, xk3, w, *rest):
    biases, out, scratch = rest[:8], rest[8], rest[9:]
    bias_s, top_s, k_s, v_s, q_s, gate_s, stat_s, sems = scratch
    step = pl.program_id(0)

    y, z, core = lax.axis_index("y"), lax.axis_index("z"), lax.axis_index("core")

    def bias_copies():
        copies = []
        for n, ref in enumerate(biases):
            slot = lax.rem(y - z + 4 + n // 2, 4)
            half = core if n % 2 == 0 else 1 - core
            at = pl.ds(pl.multiple_of(half * 256, 256), 256)
            copies.append(pltpu.make_async_copy(ref, bias_s.at[slot, :, at, :], sems.at[n]))
        return copies

    @pl.when(step == 0)
    def _():
        for copy in bias_copies():
            copy.start()
        q_s[...] = jnp.zeros_like(q_s)
        stat_s[...] = jnp.zeros_like(stat_s)
        v_s[:, :, WIDTH:, :] = jnp.ones((STEP, HEADS, PAD - WIDTH, KEYS), BF16)

    def project(r):
        x_q = xq[r]
        q_t = (matmul(w[:, :128], x_q, 0, 1) * WIDTH ** (-0.5)).astype(BF16)
        gate_s[r] = jax.nn.sigmoid(matmul(w[:, 384:], x_q, 0, 1))
        for h in range(HEADS):
            at = slice(h * WIDTH, (h + 1) * WIDTH)
            q_s[r, h, at, :] = q_t[at]
        start = 0
        for x in (xk0, xk1, xk2, xk3):
            size = x.shape[1]
            at = slice(start, start + size)
            k_s[r, at, :] = matmul(x[r], w[:, 128:256]).astype(BF16)
            v_t = matmul(w[:, 256:384], x[r], 0, 1).astype(BF16)
            for h in range(HEADS):
                v_s[r, h, :WIDTH, at] = v_t[h * WIDTH : (h + 1) * WIDTH]
            start += size

    def finish(r, totals, shifts):
        parts, stats = [], []
        for total, shift in zip(totals, shifts):
            mass = total[WIDTH : WIDTH + 1]
            parts.append(total[:WIDTH] * (1.0 / mass))
            stats.append(shift + jnp.log(mass))
        gated = jnp.concatenate(parts, axis=0) * gate_s[r]
        at = step * STEP + r
        out[:, at] = gated.T.astype(BF16).reshape(16, SHARE, CHANNELS)
        stat = jnp.concatenate(stats, axis=0)
        high = stat.astype(BF16).astype(F32)
        middle = (stat - high).astype(BF16).astype(F32)
        low = stat - high - middle
        rows = jnp.concatenate([high, middle, low, jnp.zeros_like(low)], axis=0)
        stat_s[pl.ds(pl.multiple_of(at * 32, 32), 16), :] = rows

    for r in range(STEP):
        project(r)

    @pl.when(step == 0)
    def _():
        for copy in bias_copies():
            copy.wait()
        for h in range(HEADS):
            tops = [jnp.max(bias_s[t, h], axis=0, keepdims=True) for t in range(4)]
            top = jnp.maximum(jnp.maximum(tops[0], tops[1]), jnp.maximum(tops[2], tops[3]))
            top_s[h : h + 1, :] = top.astype(F32)

    units = [(r, h, t) for r in range(STEP) for h in range(HEADS) for t in range(4)]

    def scores(r, h, t):
        at = slice(t * BLOCK, (t + 1) * BLOCK)
        return matmul(k_s[r, at, :], q_s[r, h]) + bias_s[t, h].astype(F32)

    fine, totals = [], []
    ahead, total = scores(*units[0]), None
    for n, (r, h, t) in enumerate(units):
        s, shift = ahead, top_s[h : h + 1, :]
        if n + 1 < len(units):
            ahead = scores(*units[n + 1])
        p = jnp.exp2((s - shift) * LOG2E).astype(BF16)
        pv = matmul(v_s[r, h, :, t * BLOCK : (t + 1) * BLOCK], p)
        total = pv if t == 0 else total + pv
        if t < 3:
            continue
        totals.append(total)
        if h < HEADS - 1:
            continue
        finish(r, totals, [top_s[g : g + 1, :] for g in range(HEADS)])
        mass = jnp.concatenate([total[WIDTH : WIDTH + 1] for total in totals], axis=0)
        inside = jnp.logical_and(mass > LOW, mass < HIGH)
        fine.append(jnp.min(inside.astype(F32)) > 0.5)
        totals = []

    for r in range(STEP):

        @pl.when(jnp.logical_not(fine[r]))
        def _():
            totals, shifts = [], []
            for h in range(HEADS):

                def tile(t, carry):
                    largest, total = carry
                    at = pl.ds(pl.multiple_of(t * BLOCK, BLOCK), BLOCK)
                    s = matmul(k_s[r, at, :], q_s[r, h]) + bias_s[t, h].astype(F32)
                    fresh = jnp.maximum(largest, jnp.max(s, axis=0, keepdims=True))
                    p = jnp.exp2((s - fresh) * LOG2E).astype(BF16)
                    scale = jnp.exp2((largest - fresh) * LOG2E)
                    return fresh, total * scale + matmul(v_s[r, h, :, at], p)

                begin = jnp.full((1, COLS), -jnp.inf, F32), jnp.zeros((PAD, COLS), F32)
                largest, total = lax.fori_loop(0, 4, tile, begin)
                totals.append(total)
                shifts.append(largest)
            finish(r, totals, shifts)

    @pl.when(step == pl.num_programs(0) - 1)
    def _():
        out[:, ROWS] = stat_s[...].T.astype(BF16).reshape(16, SHARE, CHANNELS)


def attend(x_q, x_ks, w_project, biases):
    def rows(x):
        return pl.BlockSpec((STEP,) + x.shape[1:], lambda i: (i, 0, 0))

    scores = ROWS * HEADS * COLS * KEYS
    message = (16, ROWS + 1, SHARE, CHANNELS)
    return pl.pallas_call(
        attend_kernel,
        grid=(ROWS // STEP,),
        in_specs=[rows(x_q)]
        + [rows(x) for x in x_ks]
        + [pl.BlockSpec((CHANNELS, 512), lambda i: (0, 0))]
        + [pl.BlockSpec(memory_space=pl.ANY)] * 8,
        out_specs=pl.BlockSpec(message, lambda i: (0, 0, 0, 0)),
        out_shape=jax.ShapeDtypeStruct(message, BF16),
        scratch_shapes=[
            pltpu.VMEM((4, HEADS, BLOCK, COLS), BF16),
            pltpu.VMEM((HEADS, COLS), F32),
            pltpu.VMEM((STEP, KEYS, CHANNELS), BF16),
            pltpu.VMEM((STEP, HEADS, PAD, KEYS), BF16),
            pltpu.VMEM((STEP, HEADS, CHANNELS, COLS), BF16),
            pltpu.VMEM((STEP, CHANNELS, COLS), F32),
            pltpu.VMEM((CHANNELS, COLS), F32),
            pltpu.SemaphoreType.DMA((8,)),
        ],
        compiler_params=pltpu.CompilerParams(vmem_limit_bytes=VMEM_LIMIT),
        cost_estimate=pl.CostEstimate(
            flops=scores * 512, bytes_accessed=2**24, transcendentals=scores
        ),
        name="attend",
    )(x_q, *x_ks, w_project, *biases)


def merge_kernel(m1, m2, w, out):
    lane = lax.broadcasted_iota(jnp.int32, (CHANNELS, CHANNELS), 0)
    head = lax.broadcasted_iota(jnp.int32, (CHANNELS, CHANNELS), 1) // WIDTH
    stat1 = m1[:, ROWS].reshape(16 * SHARE, CHANNELS)
    stat2 = jnp.concatenate([m2[s ^ 2, ROWS] for s in range(16)], axis=0)
    for i in range(ROWS):
        part = lane - 32 * i
        inside = (part >= 0) & (part < 12) & (lax.rem(part, 4) == head)
        pick = inside.astype(F32).astype(BF16)
        share = jax.nn.sigmoid(matmul(stat1, pick) - matmul(stat2, pick))
        o1 = m1[:, i].reshape(16 * SHARE, CHANNELS).astype(F32)
        o2 = jnp.concatenate([m2[s ^ 2, i] for s in range(16)], axis=0).astype(F32)
        gated = (o2 + share * (o1 - o2)).astype(BF16)
        out[:, i] = matmul(gated, w[...]).astype(BF16).reshape(16, SHARE, CHANNELS)


def merge(m1, m2, w_out):
    return pl.pallas_call(
        merge_kernel,
        out_shape=jax.ShapeDtypeStruct((16, ROWS, SHARE, CHANNELS), BF16),
        compiler_params=pltpu.CompilerParams(vmem_limit_bytes=VMEM_LIMIT),
        name="merge",
    )(m1, m2, w_out)


def shift(x, axis, step):
    return lax.ppermute(x, axis, [(i, (i + step) % 4) for i in range(4)])


def gather_direct(x, axis):
    return x, shift(x, axis, -1), shift(x, axis, 2), shift(x, axis, 1)


def gather_bias(block):
    behind, ahead = shift(block, "y", 1), shift(block, "y", -1)
    far = [shift(behind[:2], "y", 1), shift(ahead[2:], "y", -1)]
    blocks = [block, ahead, jnp.concatenate(far, axis=0), behind]
    return [side for b in blocks for side in (b, lax.ppermute(b, "core", [(0, 1), (1, 0)]))]


def shards(pair_block, norm_gain, w_project, w_out, head_bias):
    xh, xl = lax.axis_index("xh"), lax.axis_index("xl")
    own, bias_t = prepare(pair_block, norm_gain, head_bias)

    x_axis = ("xh", "xl")
    beside = lax.ppermute(own, x_axis, [(0, 1), (3, 2)])
    across = lax.ppermute(own, x_axis, [(1, 2), (2, 1)])
    first_k = jnp.where(xl == xh, own, beside)
    passed = lax.ppermute(across, x_axis, [(1, 0), (2, 3)])
    second_k = jnp.where(xl == xh, passed, across)
    partner = lax.ppermute(beside, x_axis, [(1, 2), (2, 1)])
    second_q = jnp.where(xl == xh, passed, partner)

    biases = gather_bias(bias_t)
    first_ks = gather_direct(first_k, "z")
    second_ks = gather_direct(second_k, "z")

    def spread(x):
        return lax.all_to_all(x, ROW_AXES, split_axis=0, concat_axis=0, tiled=True)

    m1 = spread(attend(own, first_ks, w_project, biases))
    m2 = spread(attend(second_q, second_ks, w_project, biases))
    update = merge(m1, m2, w_out)
    return jnp.transpose(update, (2, 0, 1, 3)).reshape(SHARE, 16 * ROWS, CHANNELS)


def solution(mesh):
    fine = Mesh(mesh.devices.reshape(4, 2, 2, 4, 2), ROW_AXES + COL_AXES)
    in_specs = (P(ROW_AXES, COL_AXES, None), P(), P(), P(), P(None, COL_AXES, ROW_AXES))
    out_specs = P(COL_AXES + ROW_AXES, None, None)
    return jax.shard_map(
        shards, mesh=fine, in_specs=in_specs, out_specs=out_specs, check_vma=False
    )
```

```python
import jax
import jax.numpy as jnp
from jax import lax
from jax.experimental import pallas as pl
from jax.experimental.pallas import tpu as pltpu
from jax.sharding import Mesh, PartitionSpec as P

F32, BF16 = jnp.float32, jnp.bfloat16
HEADS, WIDTH, CHANNELS = 4, 32, 128
COLS, BLOCK, ROWS = 512, 512, 4
KEYS = 4 * BLOCK
SHARE = COLS // 16
PAD = 40
STEP = 2
LOG2E = 1.4426950408889634
LOW, HIGH = 1e-26, 1e30
ROW_AXES = ("y", "xh", "core")
COL_AXES = ("z", "xl")
VMEM_LIMIT = 60 * 2**20


def matmul(a, b, first=1, second=0):
    dims = (((first,), (second,)), ((), ()))
    return lax.dot_general(a, b, dims, preferred_element_type=F32)


def prepare_kernel(pair, gain, bias, normed, bias_t):
    values = pair[0].astype(F32)
    centered = values - jnp.mean(values, axis=-1, keepdims=True)
    variance = jnp.mean(centered * centered, axis=-1, keepdims=True)
    normed[0] = (centered * lax.rsqrt(variance + 1e-05) * gain[...]).astype(BF16)
    bias_t[0] = bias[0].astype(F32).T.astype(BF16)


def prepare(pair_block, norm_gain, head_bias):
    def whole(*shape):
        return pl.BlockSpec((1,) + shape, lambda i: (i, 0, 0))

    keys = head_bias.shape[2]
    return pl.pallas_call(
        prepare_kernel,
        grid=(ROWS,),
        in_specs=[
            whole(COLS, CHANNELS),
            pl.BlockSpec((1, CHANNELS), lambda i: (0, 0)),
            whole(COLS, keys),
        ],
        out_specs=[whole(COLS, CHANNELS), whole(keys, COLS)],
        out_shape=[
            jax.ShapeDtypeStruct((ROWS, COLS, CHANNELS), BF16),
            jax.ShapeDtypeStruct((HEADS, keys, COLS), BF16),
        ],
        name="prepare",
    )(pair_block, norm_gain.reshape(1, CHANNELS), head_bias)


def attend_kernel(xq, xk0, xk1, xk2, xk3, w, *rest):
    biases, out, scratch = rest[:1], rest[1], rest[2:]
    bias_s, top_s, k_s, v_s, q_s, gate_s, stat_s, sems = scratch
    step = pl.program_id(0)

    z = lax.axis_index("z")

    def bias_copies():
        copies = []
        for n in range(8):
            src = biases[0].at[lax.rem(z + n // 2, 4) * 2 + n % 2]
            dst = bias_s.at[n // 2, :, pl.ds(n % 2 * 256, 256), :]
            copies.append(pltpu.make_async_copy(src, dst, sems.at[n]))
        return copies

    @pl.when(step == 0)
    def _():
        for copy in bias_copies():
            copy.start()
        q_s[...] = jnp.zeros_like(q_s)
        stat_s[...] = jnp.zeros_like(stat_s)
        v_s[:, :, WIDTH:, :] = jnp.ones((STEP, HEADS, PAD - WIDTH, KEYS), BF16)

    def project(r):
        x_q = xq[r]
        q_t = (matmul(w[:, :128], x_q, 0, 1) * WIDTH ** (-0.5)).astype(BF16)
        gate_s[r] = jax.nn.sigmoid(matmul(w[:, 384:], x_q, 0, 1))
        for h in range(HEADS):
            at = slice(h * WIDTH, (h + 1) * WIDTH)
            q_s[r, h, at, :] = q_t[at]
        start = 0
        for x in (xk0, xk1, xk2, xk3):
            size = x.shape[1]
            at = slice(start, start + size)
            k_s[r, at, :] = matmul(x[r], w[:, 128:256]).astype(BF16)
            v_t = matmul(w[:, 256:384], x[r], 0, 1).astype(BF16)
            for h in range(HEADS):
                v_s[r, h, :WIDTH, at] = v_t[h * WIDTH : (h + 1) * WIDTH]
            start += size

    def finish(r, totals, shifts):
        parts, stats = [], []
        for total, shift in zip(totals, shifts):
            mass = total[WIDTH : WIDTH + 1]
            parts.append(total[:WIDTH] * (1.0 / mass))
            stats.append(shift + jnp.log(mass))
        gated = jnp.concatenate(parts, axis=0) * gate_s[r]
        at = step * STEP + r
        out[:, at] = gated.T.astype(BF16).reshape(16, SHARE, CHANNELS)
        stat = jnp.concatenate(stats, axis=0)
        high = stat.astype(BF16).astype(F32)
        middle = (stat - high).astype(BF16).astype(F32)
        low = stat - high - middle
        rows = jnp.concatenate([high, middle, low, jnp.zeros_like(low)], axis=0)
        stat_s[pl.ds(pl.multiple_of(at * 32, 32), 16), :] = rows

    for r in range(STEP):
        project(r)

    @pl.when(step == 0)
    def _():
        for copy in bias_copies():
            copy.wait()
        for h in range(HEADS):
            tops = [jnp.max(bias_s[t, h], axis=0, keepdims=True) for t in range(4)]
            top = jnp.maximum(jnp.maximum(tops[0], tops[1]), jnp.maximum(tops[2], tops[3]))
            top_s[h : h + 1, :] = top.astype(F32)

    units = [(r, h, t) for r in range(STEP) for h in range(HEADS) for t in range(4)]

    def scores(r, h, t):
        at = slice(t * BLOCK, (t + 1) * BLOCK)
        return matmul(k_s[r, at, :], q_s[r, h]) + bias_s[t, h].astype(F32)

    fine, totals = [], []
    ahead, total = scores(*units[0]), None
    for n, (r, h, t) in enumerate(units):
        s, shift = ahead, top_s[h : h + 1, :]
        if n + 1 < len(units):
            ahead = scores(*units[n + 1])
        p = jnp.exp2((s - shift) * LOG2E).astype(BF16)
        pv = matmul(v_s[r, h, :, t * BLOCK : (t + 1) * BLOCK], p)
        total = pv if t == 0 else total + pv
        if t < 3:
            continue
        totals.append(total)
        if h < HEADS - 1:
            continue
        finish(r, totals, [top_s[g : g + 1, :] for g in range(HEADS)])
        mass = jnp.concatenate([total[WIDTH : WIDTH + 1] for total in totals], axis=0)
        inside = jnp.logical_and(mass > LOW, mass < HIGH)
        fine.append(jnp.min(inside.astype(F32)) > 0.5)
        totals = []

    for r in range(STEP):

        @pl.when(jnp.logical_not(fine[r]))
        def _():
            totals, shifts = [], []
            for h in range(HEADS):

                def tile(t, carry):
                    largest, total = carry
                    at = pl.ds(pl.multiple_of(t * BLOCK, BLOCK), BLOCK)
                    s = matmul(k_s[r, at, :], q_s[r, h]) + bias_s[t, h].astype(F32)
                    fresh = jnp.maximum(largest, jnp.max(s, axis=0, keepdims=True))
                    p = jnp.exp2((s - fresh) * LOG2E).astype(BF16)
                    scale = jnp.exp2((largest - fresh) * LOG2E)
                    return fresh, total * scale + matmul(v_s[r, h, :, at], p)

                begin = jnp.full((1, COLS), -jnp.inf, F32), jnp.zeros((PAD, COLS), F32)
                largest, total = lax.fori_loop(0, 4, tile, begin)
                totals.append(total)
                shifts.append(largest)
            finish(r, totals, shifts)

    @pl.when(step == pl.num_programs(0) - 1)
    def _():
        out[:, ROWS] = stat_s[...].T.astype(BF16).reshape(16, SHARE, CHANNELS)


def attend(x_q, x_ks, w_project, biases):
    def rows(x):
        return pl.BlockSpec((STEP,) + x.shape[1:], lambda i: (i, 0, 0))

    scores = ROWS * HEADS * COLS * KEYS
    message = (16, ROWS + 1, SHARE, CHANNELS)
    return pl.pallas_call(
        attend_kernel,
        grid=(ROWS // STEP,),
        in_specs=[rows(x_q)]
        + [rows(x) for x in x_ks]
        + [pl.BlockSpec((CHANNELS, 512), lambda i: (0, 0))]
        + [pl.BlockSpec(memory_space=pl.ANY)],
        out_specs=pl.BlockSpec(message, lambda i: (0, 0, 0, 0)),
        out_shape=jax.ShapeDtypeStruct(message, BF16),
        scratch_shapes=[
            pltpu.VMEM((4, HEADS, BLOCK, COLS), BF16),
            pltpu.VMEM((HEADS, COLS), F32),
            pltpu.VMEM((STEP, KEYS, CHANNELS), BF16),
            pltpu.VMEM((STEP, HEADS, PAD, KEYS), BF16),
            pltpu.VMEM((STEP, HEADS, CHANNELS, COLS), BF16),
            pltpu.VMEM((STEP, CHANNELS, COLS), F32),
            pltpu.VMEM((CHANNELS, COLS), F32),
            pltpu.SemaphoreType.DMA((8,)),
        ],
        compiler_params=pltpu.CompilerParams(vmem_limit_bytes=VMEM_LIMIT),
        cost_estimate=pl.CostEstimate(
            flops=scores * 512, bytes_accessed=2**24, transcendentals=scores
        ),
        name="attend",
    )(x_q, *x_ks, w_project, *biases)


def merge_kernel(m1, m2, w, out):
    lane = lax.broadcasted_iota(jnp.int32, (CHANNELS, CHANNELS), 0)
    head = lax.broadcasted_iota(jnp.int32, (CHANNELS, CHANNELS), 1) // WIDTH
    stat1 = m1[:, ROWS].reshape(16 * SHARE, CHANNELS)
    stat2 = jnp.concatenate([m2[s ^ 2, ROWS] for s in range(16)], axis=0)
    for i in range(ROWS):
        part = lane - 32 * i
        inside = (part >= 0) & (part < 12) & (lax.rem(part, 4) == head)
        pick = inside.astype(F32).astype(BF16)
        share = jax.nn.sigmoid(matmul(stat1, pick) - matmul(stat2, pick))
        o1 = m1[:, i].reshape(16 * SHARE, CHANNELS).astype(F32)
        o2 = jnp.concatenate([m2[s ^ 2, i] for s in range(16)], axis=0).astype(F32)
        gated = (o2 + share * (o1 - o2)).astype(BF16)
        out[:, i] = matmul(gated, w[...]).astype(BF16).reshape(16, SHARE, CHANNELS)


def merge(m1, m2, w_out):
    return pl.pallas_call(
        merge_kernel,
        out_shape=jax.ShapeDtypeStruct((16, ROWS, SHARE, CHANNELS), BF16),
        compiler_params=pltpu.CompilerParams(vmem_limit_bytes=VMEM_LIMIT),
        name="merge",
    )(m1, m2, w_out)


def shift(x, axis, step):
    return lax.ppermute(x, axis, [(i, (i + step) % 4) for i in range(4)])


def gather_direct(x, axis):
    return x, shift(x, axis, -1), shift(x, axis, 2), shift(x, axis, 1)


def shards(pair_block, norm_gain, w_project, w_out, head_bias):
    xh, xl = lax.axis_index("xh"), lax.axis_index("xl")
    own, bias_t = prepare(pair_block, norm_gain, head_bias)

    x_axis = ("xh", "xl")
    beside = lax.ppermute(own, x_axis, [(0, 1), (3, 2)])
    across = lax.ppermute(own, x_axis, [(1, 2), (2, 1)])
    first_k = jnp.where(xl == xh, own, beside)
    passed = lax.ppermute(across, x_axis, [(1, 0), (2, 3)])
    second_k = jnp.where(xl == xh, passed, across)
    partner = lax.ppermute(beside, x_axis, [(1, 2), (2, 1)])
    second_q = jnp.where(xl == xh, passed, partner)

    gathered = lax.all_gather(bias_t, ("y", "core"), axis=0, tiled=False)
    biases = [gathered]
    first_ks = gather_direct(first_k, "z")
    second_ks = gather_direct(second_k, "z")

    def spread(x):
        return lax.all_to_all(x, ROW_AXES, split_axis=0, concat_axis=0, tiled=True)

    m1 = spread(attend(own, first_ks, w_project, biases))
    m2 = spread(attend(second_q, second_ks, w_project, biases))
    update = merge(m1, m2, w_out)
    return jnp.transpose(update, (2, 0, 1, 3)).reshape(SHARE, 16 * ROWS, CHANNELS)


def solution(mesh):
    fine = Mesh(mesh.devices.reshape(4, 2, 2, 4, 2), ROW_AXES + COL_AXES)
    in_specs = (P(ROW_AXES, COL_AXES, None), P(), P(), P(), P(None, COL_AXES, ROW_AXES))
    out_specs = P(COL_AXES + ROW_AXES, None, None)
    return jax.shard_map(
        shards, mesh=fine, in_specs=in_specs, out_specs=out_specs, check_vma=False
    )
```

```python
import functools

import jax
import jax.numpy as jnp
from jax import lax
from jax.experimental import pallas as pl
from jax.experimental.pallas import tpu as pltpu
from jax.sharding import Mesh, PartitionSpec as P

F32, BF16 = jnp.float32, jnp.bfloat16
HEADS, WIDTH, CHANNELS = 4, 32, 128
COLS, BLOCK, ROWS = 512, 512, 4
KEYS = 4 * BLOCK
SHARE = COLS // 16
PAD = 40
STEP = 2
LOG2E = 1.4426950408889634
LOW, HIGH = 1e-26, 1e30
ROW_AXES = ("y", "xh", "core")
COL_AXES = ("z", "xl")
VMEM_LIMIT = 32 * 2**20


def matmul(a, b, first=1, second=0):
    dims = (((first,), (second,)), ((), ()))
    return lax.dot_general(a, b, dims, preferred_element_type=F32)


def prepare_kernel(pair, gain, bias, normed, bias_t):
    keys = bias.shape[2]
    places = [lax.broadcasted_iota(jnp.int32, (keys, keys), axis) for axis in (0, 1)]
    identity = (places[0] == places[1]).astype(F32).astype(BF16)
    values = pair[0].astype(F32)
    centered = values - jnp.mean(values, axis=-1, keepdims=True)
    variance = jnp.mean(centered * centered, axis=-1, keepdims=True)
    normed[0] = (centered * lax.rsqrt(variance + 1e-05) * gain[...]).astype(BF16)
    bias_t[0] = matmul(identity, bias[0], 1, 1).astype(BF16)


def prepare(pair_block, norm_gain, head_bias):
    def whole(*shape):
        return pl.BlockSpec((1,) + shape, lambda i: (i, 0, 0))

    keys = head_bias.shape[2]
    return pl.pallas_call(
        prepare_kernel,
        grid=(ROWS,),
        in_specs=[
            whole(COLS, CHANNELS),
            pl.BlockSpec((1, CHANNELS), lambda i: (0, 0)),
            whole(COLS, keys),
        ],
        out_specs=[whole(COLS, CHANNELS), whole(keys, COLS)],
        out_shape=[
            jax.ShapeDtypeStruct((ROWS, COLS, CHANNELS), BF16),
            jax.ShapeDtypeStruct((HEADS, keys, COLS), BF16),
        ],
        name="prepare",
    )(pair_block, norm_gain.reshape(1, CHANNELS), head_bias)


def attend_kernel(xq, xk0, xk1, xk2, xk3, w, *rest):
    biases, out, scratch = rest[:10], rest[-9], rest[-8:]
    bias_s, top_s, k_s, v_s, q_s, gate_s, stat_s, sems = scratch
    step = pl.program_id(0)

    y, z, core = lax.axis_index("y"), lax.axis_index("z"), lax.axis_index("core")

    def bias_copies():
        copies = []
        for n, ref in enumerate(biases):
            place = (0, 1, 3, 2, 2)[n // 2]
            heads = pl.ds((0, 0, 0, 0, 2)[n // 2], ref.shape[0])
            slot = lax.rem(y - z + 4 + place, 4)
            half = core if n % 2 == 0 else 1 - core
            at = pl.ds(pl.multiple_of(half * 256, 256), 256)
            copies.append(pltpu.make_async_copy(ref, bias_s.at[slot, heads, at, :], sems.at[n]))
        return copies

    @pl.when(step == 0)
    def _():
        for copy in bias_copies():
            copy.start()
        q_s[...] = jnp.zeros_like(q_s)
        stat_s[...] = jnp.zeros_like(stat_s)
        v_s[:, :, WIDTH:, :] = jnp.ones((STEP, HEADS, PAD - WIDTH, KEYS), BF16)

    def project(r):
        x_q = xq[r]
        q_t = (matmul(w[:, :128], x_q, 0, 1) * WIDTH ** (-0.5)).astype(BF16)
        gate_s[r] = jax.nn.sigmoid(matmul(w[:, 384:], x_q, 0, 1))
        for h in range(HEADS):
            at = slice(h * WIDTH, (h + 1) * WIDTH)
            q_s[r, h, at, :] = q_t[at]
        start = 0
        for x in (xk0, xk1, xk2, xk3):
            size = x.shape[1]
            at = slice(start, start + size)
            k_s[r, at, :] = matmul(x[r], w[:, 128:256]).astype(BF16)
            v_t = matmul(w[:, 256:384], x[r], 0, 1).astype(BF16)
            for h in range(HEADS):
                v_s[r, h, :WIDTH, at] = v_t[h * WIDTH : (h + 1) * WIDTH]
            start += size

    def finish(r, totals, shifts):
        parts, stats = [], []
        for total, shift in zip(totals, shifts):
            mass = total[WIDTH : WIDTH + 1]
            parts.append(total[:WIDTH] * (1.0 / mass))
            stats.append(shift + jnp.log(mass))
        gated = jnp.concatenate(parts, axis=0) * gate_s[r]
        at = step * STEP + r
        out[:, at] = gated.T.astype(BF16).reshape(16, SHARE, CHANNELS)
        stat = jnp.concatenate(stats, axis=0)
        high = stat.astype(BF16).astype(F32)
        middle = (stat - high).astype(BF16).astype(F32)
        low = stat - high - middle
        rows = jnp.concatenate([high, middle, low, jnp.zeros_like(low)], axis=0)
        stat_s[pl.ds(pl.multiple_of(at * 32, 32), 16), :] = rows

    for r in range(STEP):
        project(r)

    @pl.when(step == 0)
    def _():
        for copy in bias_copies():
            copy.wait()
        for h in range(HEADS):
            tops = [jnp.max(bias_s[t, h], axis=0, keepdims=True) for t in range(4)]
            top = jnp.maximum(jnp.maximum(tops[0], tops[1]), jnp.maximum(tops[2], tops[3]))
            top_s[h : h + 1, :] = top.astype(F32)

    units = [(r, h, t) for r in range(STEP) for h in range(HEADS) for t in range(4)]

    def scores(r, h, t):
        at = slice(t * BLOCK, (t + 1) * BLOCK)
        return matmul(k_s[r, at, :], q_s[r, h]) + bias_s[t, h].astype(F32)

    fine, totals = [], []
    ahead, total = scores(*units[0]), None
    for n, (r, h, t) in enumerate(units):
        s, shift = ahead, top_s[h : h + 1, :]
        if n + 1 < len(units):
            ahead = scores(*units[n + 1])
        p = jnp.exp2((s - shift) * LOG2E).astype(BF16)
        pv = matmul(v_s[r, h, :, t * BLOCK : (t + 1) * BLOCK], p)
        total = pv if t == 0 else total + pv
        if t < 3:
            continue
        totals.append(total)
        if h < HEADS - 1:
            continue
        finish(r, totals, [top_s[g : g + 1, :] for g in range(HEADS)])
        mass = jnp.concatenate([total[WIDTH : WIDTH + 1] for total in totals], axis=0)
        inside = jnp.logical_and(mass > LOW, mass < HIGH)
        fine.append(jnp.min(inside.astype(F32)) > 0.5)
        totals = []

    for r in range(STEP):

        @pl.when(jnp.logical_not(fine[r]))
        def _():
            totals, shifts = [], []
            for h in range(HEADS):

                def tile(t, carry):
                    largest, total = carry
                    at = pl.ds(pl.multiple_of(t * BLOCK, BLOCK), BLOCK)
                    s = matmul(k_s[r, at, :], q_s[r, h]) + bias_s[t, h].astype(F32)
                    fresh = jnp.maximum(largest, jnp.max(s, axis=0, keepdims=True))
                    p = jnp.exp2((s - fresh) * LOG2E).astype(BF16)
                    scale = jnp.exp2((largest - fresh) * LOG2E)
                    return fresh, total * scale + matmul(v_s[r, h, :, at], p)

                begin = jnp.full((1, COLS), -jnp.inf, F32), jnp.zeros((PAD, COLS), F32)
                largest, total = lax.fori_loop(0, 4, tile, begin)
                totals.append(total)
                shifts.append(largest)
            finish(r, totals, shifts)

    @pl.when(step == pl.num_programs(0) - 1)
    def _():
        out[:, ROWS] = stat_s[...].T.astype(BF16).reshape(16, SHARE, CHANNELS)


def attend(x_q, x_ks, w_project, biases, message=()):
    half = len(message)

    def rows(x):
        return pl.BlockSpec((STEP,) + x.shape[1:], lambda i: (i, 0, 0))

    scores = ROWS * HEADS * COLS * KEYS
    block = (16, ROWS + 1, SHARE, CHANNELS)
    return pl.pallas_call(
        attend_kernel,
        grid=(ROWS // STEP,),
        in_specs=[rows(x_q)]
        + [rows(x) for x in x_ks]
        + [pl.BlockSpec((CHANNELS, 512), lambda i: (0, 0))]
        + [pl.BlockSpec(memory_space=pl.ANY)] * (len(biases) + len(message)),
        out_specs=pl.BlockSpec(block, lambda i: (0, half, 0, 0)),
        out_shape=jax.ShapeDtypeStruct((16, 2 * (ROWS + 1), SHARE, CHANNELS), BF16),
        input_output_aliases={6 + len(biases): 0} if half else {},
        scratch_shapes=[
            pltpu.VMEM((4, HEADS, BLOCK, COLS), BF16),
            pltpu.VMEM((HEADS, COLS), F32),
            pltpu.VMEM((STEP, KEYS, CHANNELS), BF16),
            pltpu.VMEM((STEP, HEADS, PAD, KEYS), BF16),
            pltpu.VMEM((STEP, HEADS, CHANNELS, COLS), BF16),
            pltpu.VMEM((STEP, CHANNELS, COLS), F32),
            pltpu.VMEM((CHANNELS, COLS), F32),
            pltpu.SemaphoreType.DMA((10,)),
        ],
        compiler_params=pltpu.CompilerParams(vmem_limit_bytes=VMEM_LIMIT),
        cost_estimate=pl.CostEstimate(
            flops=scores * 512, bytes_accessed=2**24, transcendentals=scores
        ),
        name="attend",
    )(x_q, *x_ks, w_project, *biases, *message)


def merge_kernel(message, w, out):
    lane = lax.broadcasted_iota(jnp.int32, (CHANNELS, CHANNELS), 0)
    head = lax.broadcasted_iota(jnp.int32, (CHANNELS, CHANNELS), 1) // WIDTH
    rows = []
    for s in range(4):
        other = s ^ 2
        stat1, stat2 = message[s, ROWS], message[other, 2 * ROWS + 1]
        for i in range(ROWS):
            part = lane - 32 * i
            inside = (part >= 0) & (part < 12) & (lax.rem(part, 4) == head)
            pick = inside.astype(F32).astype(BF16)
            share = jax.nn.sigmoid(matmul(stat1, pick) - matmul(stat2, pick))
            o1 = message[s, i].astype(F32)
            o2 = message[other, ROWS + 1 + i].astype(F32)
            rows.append((o2 + share * (o1 - o2)).astype(BF16))
    update = matmul(jnp.concatenate(rows, axis=0), w[...])
    update = jnp.swapaxes(update.reshape(4 * ROWS, SHARE, CHANNELS), 0, 1)
    out[...] = update.astype(BF16)


def merge(message, w_out):
    return pl.pallas_call(
        merge_kernel,
        grid=(4,),
        in_specs=[
            pl.BlockSpec((4,) + message.shape[1:], lambda y: (y, 0, 0, 0)),
            pl.BlockSpec((CHANNELS, CHANNELS), lambda y: (0, 0)),
        ],
        out_specs=pl.BlockSpec((SHARE, 4 * ROWS, CHANNELS), lambda y: (0, y, 0)),
        out_shape=jax.ShapeDtypeStruct((SHARE, 16 * ROWS, CHANNELS), BF16),
        compiler_params=pltpu.CompilerParams(vmem_limit_bytes=VMEM_LIMIT),
        name="merge",
    )(message, w_out)


def choose(sources, picks, after=()):
    def kernel(*refs):
        ins, outs, sems = refs[: len(sources)], refs[len(sources) + len(after) : -1], refs[-1]
        place = lax.axis_index("xh") * 2 + lax.axis_index("xl")
        for act in ("start", "wait"):
            for n, pick in enumerate(picks):
                for source in sorted(set(pick)):
                    here = [place == p for p in range(4) if pick[p] == source]
                    copy = pltpu.make_async_copy(ins[source], outs[n], sems.at[n])
                    pl.when(functools.reduce(jnp.logical_or, here))(getattr(copy, act))

    anywhere = pl.BlockSpec(memory_space=pl.ANY)
    shape = jax.ShapeDtypeStruct(sources[0].shape, sources[0].dtype)
    return pl.pallas_call(
        kernel,
        in_specs=[anywhere] * (len(sources) + len(after)),
        out_specs=[anywhere] * len(picks),
        out_shape=[shape] * len(picks),
        scratch_shapes=[pltpu.SemaphoreType.DMA((len(picks),))],
        name="choose",
    )(*sources, *after)


def shift(x, axis, step):
    return lax.ppermute(x, axis, [(i, (i + step) % 4) for i in range(4)])


def swap(x):
    return lax.ppermute(x, "core", [(0, 1), (1, 0)])


def gather_bias(block):
    behind, ahead = shift(block, "y", 1), shift(block, "y", -1)
    far = [shift(behind[:2], "y", 1), shift(ahead[2:], "y", -1)]
    return [side for b in (block, ahead, behind, *far) for side in (b, swap(b))]


def shards(pair_block, norm_gain, w_project, w_out, head_bias):
    own, bias_t = prepare(pair_block, norm_gain, head_bias)
    biases = gather_bias(bias_t)

    x_axis = ("xh", "xl")
    behind, ahead = shift(own, x_axis, 1), shift(own, x_axis, -1)
    (first_k,) = choose([own, behind, ahead], [[0, 1, 2, 0]], [biases[1]])
    first_near = shift(first_k, "z", -1), shift(first_k, "z", 1)
    opposite = shift(behind, x_axis, 1)
    second_k, first_again = choose([opposite, behind, ahead, first_k], [[0, 2, 1, 0], [3] * 4])
    first_ks = first_k, first_near[0], shift(first_again, "z", 2), first_near[1]
    second_ks = second_k, shift(second_k, "z", -1), shift(second_k, "z", 2), shift(second_k, "z", 1)

    message = attend(own, first_ks, w_project, biases)
    message = attend(opposite, second_ks, w_project, biases, (message,))
    message = lax.all_to_all(message, ROW_AXES, split_axis=0, concat_axis=0, tiled=True)
    return merge(message, w_out)


def solution(mesh):
    fine = Mesh(mesh.devices.reshape(4, 2, 2, 4, 2), ROW_AXES + COL_AXES)
    in_specs = (P(ROW_AXES, COL_AXES, None), P(), P(), P(), P(None, COL_AXES, ROW_AXES))
    out_specs = P(COL_AXES + ROW_AXES, None, None)
    return jax.shard_map(
        shards, mesh=fine, in_specs=in_specs, out_specs=out_specs, check_vma=False
    )
```

```python
import jax
import jax.numpy as jnp
from jax import lax
from jax.experimental import pallas as pl
from jax.experimental.pallas import tpu as pltpu
from jax.sharding import Mesh, PartitionSpec as P

F32, BF16 = jnp.float32, jnp.bfloat16
HEADS, WIDTH, CHANNELS = 4, 32, 128
COLS, BLOCK, ROWS = 512, 512, 4
KEYS = 4 * BLOCK
SHARE = COLS // 16
PAD = 40
STEP = 2
LOG2E = 1.4426950408889634
LOW, HIGH = 1e-26, 1e30
ROW_AXES = ("y", "xh", "core")
COL_AXES = ("z", "xl")
VMEM_LIMIT = 32 * 2**20


def matmul(a, b, first=1, second=0):
    dims = (((first,), (second,)), ((), ()))
    return lax.dot_general(a, b, dims, preferred_element_type=F32)


def prepare_kernel(pair, gain, bias, normed, bias_t):
    keys = bias.shape[2]
    places = [lax.broadcasted_iota(jnp.int32, (keys, keys), axis) for axis in (0, 1)]
    identity = (places[0] == places[1]).astype(F32).astype(BF16)
    values = pair[0].astype(F32)
    centered = values - jnp.mean(values, axis=-1, keepdims=True)
    variance = jnp.mean(centered * centered, axis=-1, keepdims=True)
    normed[0] = (centered * lax.rsqrt(variance + 1e-05) * gain[...]).astype(BF16)
    bias_t[0] = matmul(identity, bias[0], 1, 1).astype(BF16)


def prepare(pair_block, norm_gain, head_bias):
    def whole(*shape):
        return pl.BlockSpec((1,) + shape, lambda i: (i, 0, 0))

    keys = head_bias.shape[2]
    return pl.pallas_call(
        prepare_kernel,
        grid=(ROWS,),
        in_specs=[
            whole(COLS, CHANNELS),
            pl.BlockSpec((1, CHANNELS), lambda i: (0, 0)),
            whole(COLS, keys),
        ],
        out_specs=[whole(COLS, CHANNELS), whole(keys, COLS)],
        out_shape=[
            jax.ShapeDtypeStruct((ROWS, COLS, CHANNELS), BF16),
            jax.ShapeDtypeStruct((HEADS, keys, COLS), BF16),
        ],
        name="prepare",
    )(pair_block, norm_gain.reshape(1, CHANNELS), head_bias)


def attend_kernel(xq, xk0, xk1, xk2, xk3, w, *rest):
    biases, out, scratch = rest[:10], rest[-9], rest[-8:]
    bias_s, top_s, k_s, v_s, q_s, gate_s, stat_s, sems = scratch
    step = pl.program_id(0)

    y, z, core = lax.axis_index("y"), lax.axis_index("z"), lax.axis_index("core")

    def bias_copies():
        copies = []
        for n, ref in enumerate(biases):
            place = (0, 1, 3, 2, 2)[n // 2]
            heads = pl.ds((0, 0, 0, 0, 2)[n // 2], ref.shape[0])
            slot = lax.rem(y - z + 4 + place, 4)
            half = core if n % 2 == 0 else 1 - core
            at = pl.ds(pl.multiple_of(half * 256, 256), 256)
            copies.append(pltpu.make_async_copy(ref, bias_s.at[slot, heads, at, :], sems.at[n]))
        return copies

    @pl.when(step == 0)
    def _():
        for copy in bias_copies():
            copy.start()
        q_s[...] = jnp.zeros_like(q_s)
        stat_s[...] = jnp.zeros_like(stat_s)
        v_s[:, :, WIDTH:, :] = jnp.ones((STEP, HEADS, PAD - WIDTH, KEYS), BF16)

    def project(r):
        x_q = xq[r]
        q_t = (matmul(w[:, :128], x_q, 0, 1) * WIDTH ** (-0.5)).astype(BF16)
        gate_s[r] = jax.nn.sigmoid(matmul(w[:, 384:], x_q, 0, 1))
        for h in range(HEADS):
            at = slice(h * WIDTH, (h + 1) * WIDTH)
            q_s[r, h, at, :] = q_t[at]
        start = 0
        for x in (xk0, xk1, xk2, xk3):
            size = x.shape[1]
            at = slice(start, start + size)
            k_s[r, at, :] = matmul(x[r], w[:, 128:256]).astype(BF16)
            v_t = matmul(w[:, 256:384], x[r], 0, 1).astype(BF16)
            for h in range(HEADS):
                v_s[r, h, :WIDTH, at] = v_t[h * WIDTH : (h + 1) * WIDTH]
            start += size

    def finish(r, totals, shifts):
        parts, stats = [], []
        for total, shift in zip(totals, shifts):
            mass = total[WIDTH : WIDTH + 1]
            parts.append(total[:WIDTH] * (1.0 / mass))
            stats.append(shift + jnp.log(mass))
        gated = jnp.concatenate(parts, axis=0) * gate_s[r]
        at = step * STEP + r
        out[:, at] = gated.T.astype(BF16).reshape(16, SHARE, CHANNELS)
        stat = jnp.concatenate(stats, axis=0)
        high = stat.astype(BF16).astype(F32)
        middle = (stat - high).astype(BF16).astype(F32)
        low = stat - high - middle
        rows = jnp.concatenate([high, middle, low, jnp.zeros_like(low)], axis=0)
        stat_s[pl.ds(pl.multiple_of(at * 32, 32), 16), :] = rows

    for r in range(STEP):
        project(r)

    @pl.when(step == 0)
    def _():
        for copy in bias_copies():
            copy.wait()
        for h in range(HEADS):
            tops = [jnp.max(bias_s[t, h], axis=0, keepdims=True) for t in range(4)]
            top = jnp.maximum(jnp.maximum(tops[0], tops[1]), jnp.maximum(tops[2], tops[3]))
            top_s[h : h + 1, :] = top.astype(F32)

    units = [(r, h, t) for r in range(STEP) for h in range(HEADS) for t in range(4)]

    def scores(r, h, t):
        at = slice(t * BLOCK, (t + 1) * BLOCK)
        return matmul(k_s[r, at, :], q_s[r, h]) + bias_s[t, h].astype(F32)

    fine, totals = [], []
    ahead, total = scores(*units[0]), None
    for n, (r, h, t) in enumerate(units):
        s, shift = ahead, top_s[h : h + 1, :]
        if n + 1 < len(units):
            ahead = scores(*units[n + 1])
        p = jnp.exp2((s - shift) * LOG2E).astype(BF16)
        pv = matmul(v_s[r, h, :, t * BLOCK : (t + 1) * BLOCK], p)
        total = pv if t == 0 else total + pv
        if t < 3:
            continue
        totals.append(total)
        if h < HEADS - 1:
            continue
        finish(r, totals, [top_s[g : g + 1, :] for g in range(HEADS)])
        mass = jnp.concatenate([total[WIDTH : WIDTH + 1] for total in totals], axis=0)
        inside = jnp.logical_and(mass > LOW, mass < HIGH)
        fine.append(jnp.min(inside.astype(F32)) > 0.5)
        totals = []

    for r in range(STEP):

        @pl.when(jnp.logical_not(fine[r]))
        def _():
            totals, shifts = [], []
            for h in range(HEADS):

                def tile(t, carry):
                    largest, total = carry
                    at = pl.ds(pl.multiple_of(t * BLOCK, BLOCK), BLOCK)
                    s = matmul(k_s[r, at, :], q_s[r, h]) + bias_s[t, h].astype(F32)
                    fresh = jnp.maximum(largest, jnp.max(s, axis=0, keepdims=True))
                    p = jnp.exp2((s - fresh) * LOG2E).astype(BF16)
                    scale = jnp.exp2((largest - fresh) * LOG2E)
                    return fresh, total * scale + matmul(v_s[r, h, :, at], p)

                begin = jnp.full((1, COLS), -jnp.inf, F32), jnp.zeros((PAD, COLS), F32)
                largest, total = lax.fori_loop(0, 4, tile, begin)
                totals.append(total)
                shifts.append(largest)
            finish(r, totals, shifts)

    @pl.when(step == pl.num_programs(0) - 1)
    def _():
        out[:, ROWS] = stat_s[...].T.astype(BF16).reshape(16, SHARE, CHANNELS)


def attend(x_q, x_ks, w_project, biases, message=()):
    half = len(message)

    def rows(x):
        return pl.BlockSpec((STEP,) + x.shape[1:], lambda i: (i, 0, 0))

    scores = ROWS * HEADS * COLS * KEYS
    block = (16, ROWS + 1, SHARE, CHANNELS)
    return pl.pallas_call(
        attend_kernel,
        grid=(ROWS // STEP,),
        in_specs=[rows(x_q)]
        + [rows(x) for x in x_ks]
        + [pl.BlockSpec((CHANNELS, 512), lambda i: (0, 0))]
        + [pl.BlockSpec(memory_space=pl.ANY)] * (len(biases) + len(message)),
        out_specs=pl.BlockSpec(block, lambda i: (0, half, 0, 0)),
        out_shape=jax.ShapeDtypeStruct((16, 2 * (ROWS + 1), SHARE, CHANNELS), BF16),
        input_output_aliases={6 + len(biases): 0} if half else {},
        scratch_shapes=[
            pltpu.VMEM((4, HEADS, BLOCK, COLS), BF16),
            pltpu.VMEM((HEADS, COLS), F32),
            pltpu.VMEM((STEP, KEYS, CHANNELS), BF16),
            pltpu.VMEM((STEP, HEADS, PAD, KEYS), BF16),
            pltpu.VMEM((STEP, HEADS, CHANNELS, COLS), BF16),
            pltpu.VMEM((STEP, CHANNELS, COLS), F32),
            pltpu.VMEM((CHANNELS, COLS), F32),
            pltpu.SemaphoreType.DMA((10,)),
        ],
        compiler_params=pltpu.CompilerParams(vmem_limit_bytes=VMEM_LIMIT),
        cost_estimate=pl.CostEstimate(
            flops=scores * 512, bytes_accessed=2**24, transcendentals=scores
        ),
        name="attend",
    )(x_q, *x_ks, w_project, *biases, *message)


def merge_kernel(message, w, out):
    lane = lax.broadcasted_iota(jnp.int32, (CHANNELS, CHANNELS), 0)
    head = lax.broadcasted_iota(jnp.int32, (CHANNELS, CHANNELS), 1) // WIDTH
    rows = []
    for s in range(4):
        other = s ^ 2
        stat1, stat2 = message[s, ROWS], message[other, 2 * ROWS + 1]
        for i in range(ROWS):
            part = lane - 32 * i
            inside = (part >= 0) & (part < 12) & (lax.rem(part, 4) == head)
            pick = inside.astype(F32).astype(BF16)
            share = jax.nn.sigmoid(matmul(stat1, pick) - matmul(stat2, pick))
            o1 = message[s, i].astype(F32)
            o2 = message[other, ROWS + 1 + i].astype(F32)
            rows.append((o2 + share * (o1 - o2)).astype(BF16))
    update = matmul(jnp.concatenate(rows, axis=0), w[...])
    update = jnp.swapaxes(update.reshape(4 * ROWS, SHARE, CHANNELS), 0, 1)
    out[...] = update.astype(BF16)


def merge(message, w_out):
    return pl.pallas_call(
        merge_kernel,
        grid=(4,),
        in_specs=[
            pl.BlockSpec((4,) + message.shape[1:], lambda y: (y, 0, 0, 0)),
            pl.BlockSpec((CHANNELS, CHANNELS), lambda y: (0, 0)),
        ],
        out_specs=pl.BlockSpec((SHARE, 4 * ROWS, CHANNELS), lambda y: (0, y, 0)),
        out_shape=jax.ShapeDtypeStruct((SHARE, 16 * ROWS, CHANNELS), BF16),
        compiler_params=pltpu.CompilerParams(vmem_limit_bytes=VMEM_LIMIT),
        name="merge",
    )(message, w_out)


def tied(x, *before):
    for array in before:
        x = x + 0 * array[(0,) * array.ndim]
    return x


def shift(x, axis, step):
    return lax.ppermute(x, axis, [(i, (i + step) % 4) for i in range(4)])


def swap(x):
    return lax.ppermute(x, "core", [(0, 1), (1, 0)])


def gather_direct(x, axis):
    return x, shift(x, axis, -1), shift(x, axis, 2), shift(x, axis, 1)


def gather_bias(block):
    behind, ahead = shift(block, "y", 1), shift(block, "y", -1)
    far = [shift(behind[:2], "y", 1), shift(ahead[2:], "y", -1)]
    return [side for b in (block, ahead, behind, *far) for side in (b, swap(b))]


def shards(pair_block, norm_gain, w_project, w_out, head_bias):
    own, bias_t = prepare(pair_block, norm_gain, head_bias)
    biases = gather_bias(bias_t)

    xh, xl = lax.axis_index("xh"), lax.axis_index("xl")
    behind, ahead = shift(own, ("xh", "xl"), 1), shift(own, ("xh", "xl"), -1)
    opposite = shift(behind, ("xh", "xl"), 1)
    near = jnp.where(xh == 0, behind, ahead)
    first_ks = gather_direct(tied(jnp.where(xl == xh, own, near), biases[1]), "z")
    near = jnp.where(xh == 0, ahead, behind)
    second_ks = gather_direct(tied(jnp.where(xl == xh, opposite, near), *first_ks[1:]), "z")

    message = attend(own, first_ks, w_project, biases)
    message = attend(opposite, second_ks, w_project, biases, (message,))
    message = lax.all_to_all(message, ROW_AXES, split_axis=0, concat_axis=0, tiled=True)
    return merge(message, w_out)


def solution(mesh):
    fine = Mesh(mesh.devices.reshape(4, 2, 2, 4, 2), ROW_AXES + COL_AXES)
    in_specs = (P(ROW_AXES, COL_AXES, None), P(), P(), P(), P(None, COL_AXES, ROW_AXES))
    out_specs = P(COL_AXES + ROW_AXES, None, None)
    return jax.shard_map(
        shards, mesh=fine, in_specs=in_specs, out_specs=out_specs, check_vma=False
    )
```

```python
import jax
import jax.numpy as jnp
from jax import lax
from jax.experimental import pallas as pl
from jax.experimental.pallas import tpu as pltpu
from jax.sharding import Mesh, PartitionSpec as P

F32, BF16 = jnp.float32, jnp.bfloat16
HEADS, WIDTH, CHANNELS = 4, 32, 128
COLS, BLOCK, ROWS = 512, 512, 4
KEYS = 4 * BLOCK
SHARE = COLS // 16
PAD = 40
PARTIAL = CHANNELS + 4 * HEADS
STEP = 2
LOG2E = 1.4426950408889634
LOW, HIGH = 1e-26, 1e30
ROW_AXES = ("y", "xh", "core")
COL_AXES = ("z", "xl")
VMEM_LIMIT = 32 * 2**20


def matmul(a, b, first=1, second=0):
    dims = (((first,), (second,)), ((), ()))
    return lax.dot_general(a, b, dims, preferred_element_type=F32)


def prepare_kernel(pair, gain, bias, normed, bias_t):
    keys = bias.shape[2]
    places = [lax.broadcasted_iota(jnp.int32, (keys, keys), axis) for axis in (0, 1)]
    identity = (places[0] == places[1]).astype(F32).astype(BF16)
    values = pair[0].astype(F32)
    centered = values - jnp.mean(values, axis=-1, keepdims=True)
    variance = jnp.mean(centered * centered, axis=-1, keepdims=True)
    normed[0] = (centered * lax.rsqrt(variance + 1e-05) * gain[...]).astype(BF16)
    bias_t[0] = matmul(identity, bias[0], 1, 1).astype(BF16)


def prepare(pair_block, norm_gain, head_bias):
    def whole(*shape):
        return pl.BlockSpec((1,) + shape, lambda i: (i, 0, 0))

    keys = head_bias.shape[2]
    return pl.pallas_call(
        prepare_kernel,
        grid=(ROWS,),
        in_specs=[
            whole(COLS, CHANNELS),
            pl.BlockSpec((1, CHANNELS), lambda i: (0, 0)),
            whole(COLS, keys),
        ],
        out_specs=[whole(COLS, CHANNELS), whole(keys, COLS)],
        out_shape=[
            jax.ShapeDtypeStruct((ROWS, COLS, CHANNELS), BF16),
            jax.ShapeDtypeStruct((HEADS, keys, COLS), BF16),
        ],
        name="prepare",
    )(pair_block, norm_gain.reshape(1, CHANNELS), head_bias)


def attend_kernel(xq, xk0, xk1, xk2, xk3, w, *rest):
    biases, out, (bias_s, top_s, k_s, v_s, q_s, sems) = rest[:10], rest[10], rest[11:]
    step = pl.program_id(0)
    y, z, core = lax.axis_index("y"), lax.axis_index("z"), lax.axis_index("core")

    def bias_copies():
        copies = []
        for n, ref in enumerate(biases):
            place = (0, 1, 3, 2, 2)[n // 2]
            heads = pl.ds((0, 0, 0, 0, 2)[n // 2], ref.shape[0])
            slot = lax.rem(y - z + 4 + place, 4)
            half = core if n % 2 == 0 else 1 - core
            at = pl.ds(pl.multiple_of(half * 256, 256), 256)
            copies.append(pltpu.make_async_copy(ref, bias_s.at[slot, heads, at, :], sems.at[n]))
        return copies

    @pl.when(step == 0)
    def _():
        for copy in bias_copies():
            copy.start()
        q_s[...] = jnp.zeros_like(q_s)
        v_s[:, :, WIDTH:, :] = jnp.ones((STEP, HEADS, PAD - WIDTH, KEYS), BF16)

    def project(r):
        x_q = xq[r]
        q_t = (matmul(w[:, :128], x_q, 0, 1) * WIDTH ** (-0.5)).astype(BF16)
        for h in range(HEADS):
            at = slice(h * WIDTH, (h + 1) * WIDTH)
            q_s[r, h, at, :] = q_t[at]
        start = 0
        for x in (xk0, xk1, xk2, xk3):
            size = x.shape[1]
            at = slice(start, start + size)
            k_s[r, at, :] = matmul(x[r], w[:, 128:256]).astype(BF16)
            v_t = matmul(w[:, 256:384], x[r], 0, 1).astype(BF16)
            for h in range(HEADS):
                v_s[r, h, :WIDTH, at] = v_t[h * WIDTH : (h + 1) * WIDTH]
            start += size

    def finish(r, totals, shifts):
        parts, stats = [], []
        for total, shift in zip(totals, shifts):
            mass = total[WIDTH : WIDTH + 1]
            parts.append(total[:WIDTH] * (1.0 / mass))
            stats.append(shift + jnp.log(mass))
        stat = jnp.concatenate(stats, axis=0)
        high = stat.astype(BF16).astype(F32)
        middle = (stat - high).astype(BF16).astype(F32)
        low = stat - high - middle
        rows = parts + [high, middle, low, jnp.zeros_like(low)]
        out[r] = jnp.concatenate(rows, axis=0).astype(out.dtype)

    for r in range(STEP):
        project(r)

    @pl.when(step == 0)
    def _():
        for copy in bias_copies():
            copy.wait()
        for h in range(HEADS):
            tops = [jnp.max(bias_s[t, h], axis=0, keepdims=True) for t in range(4)]
            top = jnp.maximum(jnp.maximum(tops[0], tops[1]), jnp.maximum(tops[2], tops[3]))
            top_s[h : h + 1, :] = top.astype(F32)

    units = [(r, h, t) for r in range(STEP) for h in range(HEADS) for t in range(4)]

    def scores(r, h, t):
        at = slice(t * BLOCK, (t + 1) * BLOCK)
        return matmul(k_s[r, at, :], q_s[r, h]) + bias_s[t, h].astype(F32)

    fine, totals = [], []
    ahead, total = scores(*units[0]), None
    for n, (r, h, t) in enumerate(units):
        s, shift = ahead, top_s[h : h + 1, :]
        if n + 1 < len(units):
            ahead = scores(*units[n + 1])
        p = jnp.exp2((s - shift) * LOG2E).astype(BF16)
        pv = matmul(v_s[r, h, :, t * BLOCK : (t + 1) * BLOCK], p)
        total = pv if t == 0 else total + pv
        if t < 3:
            continue
        totals.append(total)
        if h < HEADS - 1:
            continue
        finish(r, totals, [top_s[g : g + 1, :] for g in range(HEADS)])
        mass = jnp.concatenate([total[WIDTH : WIDTH + 1] for total in totals], axis=0)
        inside = jnp.logical_and(mass > LOW, mass < HIGH)
        fine.append(jnp.min(inside.astype(F32)) > 0.5)
        totals = []

    for r in range(STEP):

        @pl.when(jnp.logical_not(fine[r]))
        def _():
            totals, shifts = [], []
            for h in range(HEADS):

                def tile(t, carry):
                    largest, total = carry
                    at = pl.ds(pl.multiple_of(t * BLOCK, BLOCK), BLOCK)
                    s = matmul(k_s[r, at, :], q_s[r, h]) + bias_s[t, h].astype(F32)
                    fresh = jnp.maximum(largest, jnp.max(s, axis=0, keepdims=True))
                    p = jnp.exp2((s - fresh) * LOG2E).astype(BF16)
                    scale = jnp.exp2((largest - fresh) * LOG2E)
                    return fresh, total * scale + matmul(v_s[r, h, :, at], p)

                begin = jnp.full((1, COLS), -jnp.inf, F32), jnp.zeros((PAD, COLS), F32)
                largest, total = lax.fori_loop(0, 4, tile, begin)
                totals.append(total)
                shifts.append(largest)
            finish(r, totals, shifts)


def attend(x_q, x_ks, w_project, biases, dtype):
    def rows(x):
        return pl.BlockSpec((STEP,) + x.shape[1:], lambda i: (i, 0, 0))

    scores = ROWS * HEADS * COLS * KEYS
    return pl.pallas_call(
        attend_kernel,
        grid=(ROWS // STEP,),
        in_specs=[rows(x_q)]
        + [rows(x) for x in x_ks]
        + [pl.BlockSpec((CHANNELS, 512), lambda i: (0, 0))]
        + [pl.BlockSpec(memory_space=pl.ANY)] * len(biases),
        out_specs=pl.BlockSpec((STEP, PARTIAL, COLS), lambda i: (i, 0, 0)),
        out_shape=jax.ShapeDtypeStruct((ROWS, PARTIAL, COLS), dtype),
        scratch_shapes=[
            pltpu.VMEM((4, HEADS, BLOCK, COLS), BF16),
            pltpu.VMEM((HEADS, COLS), F32),
            pltpu.VMEM((STEP, KEYS, CHANNELS), BF16),
            pltpu.VMEM((STEP, HEADS, PAD, KEYS), BF16),
            pltpu.VMEM((STEP, HEADS, CHANNELS, COLS), BF16),
            pltpu.SemaphoreType.DMA((10,)),
        ],
        compiler_params=pltpu.CompilerParams(vmem_limit_bytes=VMEM_LIMIT),
        cost_estimate=pl.CostEstimate(
            flops=scores * 512, bytes_accessed=2**24, transcendentals=scores
        ),
        name="attend",
    )(x_q, *x_ks, w_project, *biases)


def update_kernel(x, w, w_out, mine, theirs, out):
    def parts(partial):
        p = partial[0].astype(F32)
        stat = p[CHANNELS : CHANNELS + 4] + p[CHANNELS + 4 : CHANNELS + 8]
        return p[:CHANNELS], stat + p[CHANNELS + 8 : CHANNELS + 12]

    (o1, stat1), (o2, stat2) = parts(mine), parts(theirs)
    share = jax.nn.sigmoid(stat1 - stat2)
    lines = [jnp.broadcast_to(share[h : h + 1], (WIDTH, COLS)) for h in range(HEADS)]
    attended = o2 + jnp.concatenate(lines, axis=0) * (o1 - o2)
    gate = jax.nn.sigmoid(matmul(w[:, 384:], x[0], 0, 1))
    gated = (gate * attended).astype(BF16)
    update = matmul(gated, w_out[...], 0, 0).astype(BF16)
    out[:, 0] = update.reshape(16, SHARE, CHANNELS)


def update_rows(x, w_project, w_out, mine, theirs):
    def row(a):
        return pl.BlockSpec((1,) + a.shape[1:], lambda i: (i, 0, 0))

    def whole(a):
        return pl.BlockSpec(a.shape, lambda i: (0, 0))

    return pl.pallas_call(
        update_kernel,
        grid=(ROWS,),
        in_specs=[row(x), whole(w_project), whole(w_out), row(mine), row(theirs)],
        out_specs=pl.BlockSpec((16, 1, SHARE, CHANNELS), lambda i: (0, i, 0, 0)),
        out_shape=jax.ShapeDtypeStruct((16, ROWS, SHARE, CHANNELS), BF16),
        compiler_params=pltpu.CompilerParams(vmem_limit_bytes=VMEM_LIMIT),
        name="update",
    )(x, w_project, w_out, mine, theirs)


def reorder_kernel(update, out):
    rows = update[...].astype(F32).reshape(4 * ROWS, SHARE, CHANNELS)
    out[...] = jnp.swapaxes(rows, 0, 1).astype(BF16)


def reorder(update):
    return pl.pallas_call(
        reorder_kernel,
        grid=(4,),
        in_specs=[pl.BlockSpec((4,) + update.shape[1:], lambda y: (y, 0, 0, 0))],
        out_specs=pl.BlockSpec((SHARE, 4 * ROWS, CHANNELS), lambda y: (0, y, 0)),
        out_shape=jax.ShapeDtypeStruct((SHARE, 16 * ROWS, CHANNELS), BF16),
        name="reorder",
    )(update)


def tied(x, *before):
    for array in before:
        x = x + 0 * array[(0,) * array.ndim]
    return x


def shift(x, axis, step):
    return lax.ppermute(x, axis, [(i, (i + step) % 4) for i in range(4)])


def swap(x):
    return lax.ppermute(x, "core", [(0, 1), (1, 0)])


def gather_direct(x, axis):
    return x, shift(x, axis, -1), shift(x, axis, 2), shift(x, axis, 1)


def gather_bias(block):
    behind, ahead = shift(block, "y", 1), shift(block, "y", -1)
    far = [shift(behind[:2], "y", 1), shift(ahead[2:], "y", -1)]
    return [side for b in (block, ahead, behind, *far) for side in (b, swap(b))]


def shards(pair_block, norm_gain, w_project, w_out, head_bias):
    own, bias_t = prepare(pair_block, norm_gain, head_bias)
    biases = gather_bias(bias_t)

    xh, xl = lax.axis_index("xh"), lax.axis_index("xl")
    opposite = lax.ppermute(own, "xh", [(0, 1), (1, 0)])
    across = lax.ppermute(own, ("xh", "xl"), [(1, 2), (2, 1)])
    beside = lax.ppermute(own, ("xh", "xl"), [(0, 1), (3, 2)])
    their_k = tied(jnp.where(xl == xh, opposite, across), biases[1])
    their_ks = gather_direct(their_k, "z")
    own_k = tied(jnp.where(xl == xh, own, beside), *their_ks[1:])
    own_ks = gather_direct(own_k, "z")

    theirs = attend(opposite, their_ks, w_project, biases, BF16)
    theirs = lax.ppermute(theirs, "xh", [(0, 1), (1, 0)])
    mine = attend(own, own_ks, w_project, biases, F32)
    update = update_rows(own, w_project, w_out, mine, theirs)
    return reorder(lax.all_to_all(update, ROW_AXES, split_axis=0, concat_axis=0, tiled=True))


def solution(mesh):
    fine = Mesh(mesh.devices.reshape(4, 2, 2, 4, 2), ROW_AXES + COL_AXES)
    in_specs = (P(ROW_AXES, COL_AXES, None), P(), P(), P(), P(None, COL_AXES, ROW_AXES))
    out_specs = P(COL_AXES + ROW_AXES, None, None)
    return jax.shard_map(
        shards, mesh=fine, in_specs=in_specs, out_specs=out_specs, check_vma=False
    )
```

```python
import functools

import jax
import jax.numpy as jnp
from jax import lax
from jax.experimental import pallas as pl
from jax.experimental.pallas import tpu as pltpu
from jax.sharding import Mesh, PartitionSpec as P

F32, BF16 = jnp.float32, jnp.bfloat16
HEADS, WIDTH, CHANNELS = 4, 32, 128
COLS, BLOCK, ROWS = 512, 512, 4
KEYS = 4 * BLOCK
SHARE = COLS // 16
PAD = 40
PARTIAL = CHANNELS + 4 * HEADS
STEP = 2
LOG2E = 1.4426950408889634
LOW, HIGH = 1e-26, 1e30
ROW_AXES = ("y", "xh", "core")
COL_AXES = ("z", "xl")
VMEM_LIMIT = 32 * 2**20


def matmul(a, b, first=1, second=0):
    dims = (((first,), (second,)), ((), ()))
    return lax.dot_general(a, b, dims, preferred_element_type=F32)


def prepare_kernel(pair, gain, bias, normed, bias_t):
    keys = bias.shape[2]
    places = [lax.broadcasted_iota(jnp.int32, (keys, keys), axis) for axis in (0, 1)]
    identity = (places[0] == places[1]).astype(F32).astype(BF16)
    values = pair[...].astype(F32)
    centered = values - jnp.mean(values, axis=-1, keepdims=True)
    variance = jnp.mean(centered * centered, axis=-1, keepdims=True)
    normed[...] = (centered * lax.rsqrt(variance + 1e-05) * gain[...]).astype(BF16)
    for h in range(bias.shape[0]):
        bias_t[h] = matmul(identity, bias[h], 1, 1).astype(BF16)


def prepare(pair_block, norm_gain, head_bias):
    def whole(*shape):
        return pl.BlockSpec((2,) + shape, lambda i: (i, 0, 0))

    keys = head_bias.shape[2]
    return pl.pallas_call(
        prepare_kernel,
        grid=(ROWS // 2,),
        in_specs=[
            whole(COLS, CHANNELS),
            pl.BlockSpec((1, CHANNELS), lambda i: (0, 0)),
            whole(COLS, keys),
        ],
        out_specs=[whole(COLS, CHANNELS), whole(keys, COLS)],
        out_shape=[
            jax.ShapeDtypeStruct((ROWS, COLS, CHANNELS), BF16),
            jax.ShapeDtypeStruct((HEADS, keys, COLS), BF16),
        ],
        name="prepare",
    )(pair_block, norm_gain.reshape(1, CHANNELS), head_bias)


def attend_kernel(blocks, xq, *rest):
    xks, w, rest = rest[:blocks], rest[blocks], rest[blocks + 1 :]
    biases, out, (bias_s, top_s, k_s, v_s, q_s, sems) = rest[:10], rest[10], rest[11:]
    step = pl.program_id(0)
    y, z, core = lax.axis_index("y"), lax.axis_index("z"), lax.axis_index("core")

    def bias_copies():
        copies = []
        for n, ref in enumerate(biases):
            place = (0, 1, 3, 2, 2)[n // 2]
            heads = pl.ds((0, 0, 0, 0, 2)[n // 2], ref.shape[0])
            slot = lax.rem(y - z + 4 + place, 4)
            half = core if n % 2 == 0 else 1 - core
            at = pl.ds(pl.multiple_of(half * 256, 256), 256)
            copies.append(pltpu.make_async_copy(ref, bias_s.at[slot, heads, at, :], sems.at[n]))
        return copies

    @pl.when(step == 0)
    def _():
        for copy in bias_copies():
            copy.start()
        q_s[...] = jnp.zeros_like(q_s)
        v_s[:, :, WIDTH:, :] = jnp.ones((STEP, HEADS, PAD - WIDTH, KEYS), BF16)

    def project(r):
        x_q = xq[r]
        q_t = (matmul(w[:, :128], x_q, 0, 1) * WIDTH ** (-0.5)).astype(BF16)
        for h in range(HEADS):
            at = slice(h * WIDTH, (h + 1) * WIDTH)
            q_s[r, h, at, :] = q_t[at]
        start = 0
        for x in xks:
            size = x.shape[1]
            at = slice(start, start + size)
            k_s[r, at, :] = matmul(x[r], w[:, 128:256]).astype(BF16)
            v_t = matmul(w[:, 256:384], x[r], 0, 1).astype(BF16)
            for h in range(HEADS):
                v_s[r, h, :WIDTH, at] = v_t[h * WIDTH : (h + 1) * WIDTH]
            start += size

    def finish(r, totals, shifts):
        parts, stats = [], []
        for total, shift in zip(totals, shifts):
            mass = total[WIDTH : WIDTH + 1]
            parts.append(total[:WIDTH] * (1.0 / mass))
            stats.append(shift + jnp.log(mass))
        stat = jnp.concatenate(stats, axis=0)
        high = stat.astype(BF16).astype(F32)
        middle = (stat - high).astype(BF16).astype(F32)
        low = stat - high - middle
        rows = parts + [high, middle, low, jnp.zeros_like(low)]
        out[r] = jnp.concatenate(rows, axis=0).astype(out.dtype)

    for r in range(STEP):
        project(r)

    @pl.when(step == 0)
    def _():
        for copy in bias_copies():
            copy.wait()
        for h in range(HEADS):
            tops = [jnp.max(bias_s[t, h], axis=0, keepdims=True) for t in range(4)]
            top = jnp.maximum(jnp.maximum(tops[0], tops[1]), jnp.maximum(tops[2], tops[3]))
            top_s[h : h + 1, :] = top.astype(F32)

    units = [(r, h, t) for r in range(STEP) for h in range(HEADS) for t in range(4)]

    def scores(r, h, t):
        at = slice(t * BLOCK, (t + 1) * BLOCK)
        return matmul(k_s[r, at, :], q_s[r, h]) + bias_s[t, h].astype(F32)

    fine, totals = [], []
    ahead, total = scores(*units[0]), None
    for n, (r, h, t) in enumerate(units):
        s, shift = ahead, top_s[h : h + 1, :]
        if n + 1 < len(units):
            ahead = scores(*units[n + 1])
        p = jnp.exp2((s - shift) * LOG2E).astype(BF16)
        pv = matmul(v_s[r, h, :, t * BLOCK : (t + 1) * BLOCK], p)
        total = pv if t == 0 else total + pv
        if t < 3:
            continue
        totals.append(total)
        if h < HEADS - 1:
            continue
        finish(r, totals, [top_s[g : g + 1, :] for g in range(HEADS)])
        mass = jnp.concatenate([total[WIDTH : WIDTH + 1] for total in totals], axis=0)
        inside = jnp.logical_and(mass > LOW, mass < HIGH)
        fine.append(jnp.min(inside.astype(F32)) > 0.5)
        totals = []

    for r in range(STEP):

        @pl.when(jnp.logical_not(fine[r]))
        def _():
            totals, shifts = [], []
            for h in range(HEADS):

                def tile(t, carry):
                    largest, total = carry
                    at = pl.ds(pl.multiple_of(t * BLOCK, BLOCK), BLOCK)
                    s = matmul(k_s[r, at, :], q_s[r, h]) + bias_s[t, h].astype(F32)
                    fresh = jnp.maximum(largest, jnp.max(s, axis=0, keepdims=True))
                    p = jnp.exp2((s - fresh) * LOG2E).astype(BF16)
                    scale = jnp.exp2((largest - fresh) * LOG2E)
                    return fresh, total * scale + matmul(v_s[r, h, :, at], p)

                begin = jnp.full((1, COLS), -jnp.inf, F32), jnp.zeros((PAD, COLS), F32)
                largest, total = lax.fori_loop(0, 4, tile, begin)
                totals.append(total)
                shifts.append(largest)
            finish(r, totals, shifts)


def attend(x_q, x_ks, w_project, biases, dtype):
    def rows(x):
        return pl.BlockSpec((STEP,) + x.shape[1:], lambda i: (i, 0, 0))

    scores = ROWS * HEADS * COLS * KEYS
    return pl.pallas_call(
        functools.partial(attend_kernel, len(x_ks)),
        grid=(ROWS // STEP,),
        in_specs=[rows(x_q)]
        + [rows(x) for x in x_ks]
        + [pl.BlockSpec((CHANNELS, 512), lambda i: (0, 0))]
        + [pl.BlockSpec(memory_space=pl.ANY)] * len(biases),
        out_specs=pl.BlockSpec((STEP, PARTIAL, COLS), lambda i: (i, 0, 0)),
        out_shape=jax.ShapeDtypeStruct((ROWS, PARTIAL, COLS), dtype),
        scratch_shapes=[
            pltpu.VMEM((4, HEADS, BLOCK, COLS), BF16),
            pltpu.VMEM((HEADS, COLS), F32),
            pltpu.VMEM((STEP, KEYS, CHANNELS), BF16),
            pltpu.VMEM((STEP, HEADS, PAD, KEYS), BF16),
            pltpu.VMEM((STEP, HEADS, CHANNELS, COLS), BF16),
            pltpu.SemaphoreType.DMA((10,)),
        ],
        compiler_params=pltpu.CompilerParams(vmem_limit_bytes=VMEM_LIMIT),
        cost_estimate=pl.CostEstimate(
            flops=scores * 512, bytes_accessed=2**24, transcendentals=scores
        ),
        name="attend",
    )(x_q, *x_ks, w_project, *biases)


def update_kernel(x, w, w_out, mine, theirs, out):
    def parts(partial):
        p = partial[0].astype(F32)
        stat = p[CHANNELS : CHANNELS + 4] + p[CHANNELS + 4 : CHANNELS + 8]
        return p[:CHANNELS], stat + p[CHANNELS + 8 : CHANNELS + 12]

    (o1, stat1), (o2, stat2) = parts(mine), parts(theirs)
    share = jax.nn.sigmoid(stat1 - stat2)
    lines = [jnp.broadcast_to(share[h : h + 1], (WIDTH, COLS)) for h in range(HEADS)]
    attended = o2 + jnp.concatenate(lines, axis=0) * (o1 - o2)
    gate = jax.nn.sigmoid(matmul(w[:, 384:], x[0], 0, 1))
    gated = (gate * attended).astype(BF16)
    update = matmul(gated, w_out[...], 0, 0).astype(BF16)
    out[:, 0] = update.reshape(16, SHARE, CHANNELS)


def update_rows(x, w_project, w_out, mine, theirs):
    def row(a):
        return pl.BlockSpec((1,) + a.shape[1:], lambda i: (i, 0, 0))

    def whole(a):
        return pl.BlockSpec(a.shape, lambda i: (0, 0))

    return pl.pallas_call(
        update_kernel,
        grid=(ROWS,),
        in_specs=[row(x), whole(w_project), whole(w_out), row(mine), row(theirs)],
        out_specs=pl.BlockSpec((16, 1, SHARE, CHANNELS), lambda i: (0, i, 0, 0)),
        out_shape=jax.ShapeDtypeStruct((16, ROWS, SHARE, CHANNELS), BF16),
        compiler_params=pltpu.CompilerParams(vmem_limit_bytes=VMEM_LIMIT),
        name="update",
    )(x, w_project, w_out, mine, theirs)


def tied(x, *before):
    for array in before:
        x = x + 0 * array[(0,) * array.ndim]
    return x


def shift(x, axis, step):
    return lax.ppermute(x, axis, [(i, (i + step) % 4) for i in range(4)])


def swap(x):
    return lax.ppermute(x, "core", [(0, 1), (1, 0)])


def gather_direct(x, axis):
    far = shift(x, axis, 2)
    return x, shift(x, axis, -1), far, shift(x, axis, 1)


def gather_ring(x, axis):
    behind, ahead = shift(x, axis, 1), shift(x, axis, -1)
    parts = tied(behind[:, :256], ahead), tied(ahead[:, 256:], behind)
    far = shift(parts[0], axis, 1), shift(parts[1], axis, -1)
    return x, ahead, *far, behind


def shards(pair_block, norm_gain, w_project, w_out, head_bias):
    own, bias_t = prepare(pair_block, norm_gain, head_bias)
    bias_own = bias_t, swap(bias_t)
    behind, ahead = shift(bias_t, "y", 1), shift(bias_t, "y", -1)

    xh, xl = lax.axis_index("xh"), lax.axis_index("xl")
    opposite = lax.ppermute(own, "xh", [(0, 1), (1, 0)])
    across = lax.ppermute(own, ("xh", "xl"), [(1, 2), (2, 1)])
    beside = lax.ppermute(own, ("xh", "xl"), [(0, 1), (3, 2)])
    their_k = tied(jnp.where(xl == xh, opposite, across), bias_own[1])
    their_ks = gather_ring(their_k, "z")
    own_k = tied(jnp.where(xl == xh, own, beside), their_ks[1], their_ks[4])
    own_ks = gather_direct(own_k, "z")

    far = shift(behind[:2], "y", 1), shift(ahead[2:], "y", -1)
    biases = [*bias_own]
    for block in (ahead, behind, *far):
        biases += [block, swap(block)]

    theirs = attend(opposite, their_ks, w_project, biases, BF16)
    theirs = lax.ppermute(theirs, "xh", [(0, 1), (1, 0)])
    mine = attend(own, own_ks, w_project, biases, F32)
    update = update_rows(own, w_project, w_out, mine, theirs)
    update = lax.all_to_all(update, ROW_AXES, split_axis=0, concat_axis=0, tiled=True)
    return jnp.transpose(update, (2, 0, 1, 3)).reshape(SHARE, 16 * ROWS, CHANNELS)


def solution(mesh):
    fine = Mesh(mesh.devices.reshape(4, 2, 2, 4, 2), ROW_AXES + COL_AXES)
    in_specs = (P(ROW_AXES, COL_AXES, None), P(), P(), P(), P(None, COL_AXES, ROW_AXES))
    out_specs = P(COL_AXES + ROW_AXES, None, None)
    return jax.shard_map(
        shards, mesh=fine, in_specs=in_specs, out_specs=out_specs, check_vma=False
    )
```

```python
import functools

import jax
import jax.numpy as jnp
from jax import lax
from jax.experimental import pallas as pl
from jax.experimental.pallas import tpu as pltpu
from jax.sharding import Mesh, PartitionSpec as P

F32, BF16 = jnp.float32, jnp.bfloat16
HEADS, WIDTH, CHANNELS = 4, 32, 128
COLS, BLOCK, ROWS = 512, 512, 4
KEYS = 4 * BLOCK
SHARE = COLS // 16
PAD = 40
PARTIAL = CHANNELS + 4 * HEADS
STEP = 2
LOG2E = 1.4426950408889634
LOW, HIGH = 1e-26, 1e30
ROW_AXES = ("y", "xh", "core")
COL_AXES = ("z", "xl")
VMEM_LIMIT = 32 * 2**20


def matmul(a, b, first=1, second=0):
    dims = (((first,), (second,)), ((), ()))
    return lax.dot_general(a, b, dims, preferred_element_type=F32)


def prepare_kernel(pair, gain, bias, normed, bias_t):
    keys = bias.shape[2]
    places = [lax.broadcasted_iota(jnp.int32, (keys, keys), axis) for axis in (0, 1)]
    identity = (places[0] == places[1]).astype(F32).astype(BF16)
    values = pair[...].astype(F32)
    centered = values - jnp.mean(values, axis=-1, keepdims=True)
    variance = jnp.mean(centered * centered, axis=-1, keepdims=True)
    normed[...] = (centered * lax.rsqrt(variance + 1e-05) * gain[...]).astype(BF16)
    for h in range(bias.shape[0]):
        bias_t[h] = matmul(identity, bias[h], 1, 1).astype(BF16)


def prepare(pair_block, norm_gain, head_bias):
    def whole(*shape):
        return pl.BlockSpec((2,) + shape, lambda i: (i, 0, 0))

    keys = head_bias.shape[2]
    return pl.pallas_call(
        prepare_kernel,
        grid=(ROWS // 2,),
        in_specs=[
            whole(COLS, CHANNELS),
            pl.BlockSpec((1, CHANNELS), lambda i: (0, 0)),
            whole(COLS, keys),
        ],
        out_specs=[whole(COLS, CHANNELS), whole(keys, COLS)],
        out_shape=[
            jax.ShapeDtypeStruct((ROWS, COLS, CHANNELS), BF16),
            jax.ShapeDtypeStruct((HEADS, keys, COLS), BF16),
        ],
        name="prepare",
    )(pair_block, norm_gain.reshape(1, CHANNELS), head_bias)


def attend_kernel(blocks, xq, *rest):
    xks, w, rest = rest[:blocks], rest[blocks], rest[blocks + 1 :]
    biases, out, (bias_s, top_s, k_s, v_s, q_s, sems) = rest[:1], rest[1], rest[2:]
    step = pl.program_id(0)
    z = lax.axis_index("z")

    def bias_copies():
        copies = []
        for n in range(8):
            src = biases[0].at[lax.rem(z + n // 2, 4) * 2 + n % 2]
            dst = bias_s.at[n // 2, :, pl.ds(n % 2 * 256, 256), :]
            copies.append(pltpu.make_async_copy(src, dst, sems.at[n]))
        return copies

    @pl.when(step == 0)
    def _():
        for copy in bias_copies():
            copy.start()
        q_s[...] = jnp.zeros_like(q_s)
        v_s[:, :, WIDTH:, :] = jnp.ones((STEP, HEADS, PAD - WIDTH, KEYS), BF16)

    def project(r):
        x_q = xq[r]
        q_t = (matmul(w[:, :128], x_q, 0, 1) * WIDTH ** (-0.5)).astype(BF16)
        for h in range(HEADS):
            at = slice(h * WIDTH, (h + 1) * WIDTH)
            q_s[r, h, at, :] = q_t[at]
        start = 0
        for x in xks:
            size = x.shape[1]
            at = slice(start, start + size)
            k_s[r, at, :] = matmul(x[r], w[:, 128:256]).astype(BF16)
            v_t = matmul(w[:, 256:384], x[r], 0, 1).astype(BF16)
            for h in range(HEADS):
                v_s[r, h, :WIDTH, at] = v_t[h * WIDTH : (h + 1) * WIDTH]
            start += size

    def finish(r, totals, shifts):
        parts, stats = [], []
        for total, shift in zip(totals, shifts):
            mass = total[WIDTH : WIDTH + 1]
            parts.append(total[:WIDTH] * (1.0 / mass))
            stats.append(shift + jnp.log(mass))
        stat = jnp.concatenate(stats, axis=0)
        high = stat.astype(BF16).astype(F32)
        middle = (stat - high).astype(BF16).astype(F32)
        low = stat - high - middle
        rows = parts + [high, middle, low, jnp.zeros_like(low)]
        out[r] = jnp.concatenate(rows, axis=0).astype(out.dtype)

    for r in range(STEP):
        project(r)

    @pl.when(step == 0)
    def _():
        for copy in bias_copies():
            copy.wait()
        for h in range(HEADS):
            tops = [jnp.max(bias_s[t, h], axis=0, keepdims=True) for t in range(4)]
            top = jnp.maximum(jnp.maximum(tops[0], tops[1]), jnp.maximum(tops[2], tops[3]))
            top_s[h : h + 1, :] = top.astype(F32)

    units = [(r, h, t) for r in range(STEP) for h in range(HEADS) for t in range(4)]

    def scores(r, h, t):
        at = slice(t * BLOCK, (t + 1) * BLOCK)
        return matmul(k_s[r, at, :], q_s[r, h]) + bias_s[t, h].astype(F32)

    fine, totals = [], []
    ahead, total = scores(*units[0]), None
    for n, (r, h, t) in enumerate(units):
        s, shift = ahead, top_s[h : h + 1, :]
        if n + 1 < len(units):
            ahead = scores(*units[n + 1])
        p = jnp.exp2((s - shift) * LOG2E).astype(BF16)
        pv = matmul(v_s[r, h, :, t * BLOCK : (t + 1) * BLOCK], p)
        total = pv if t == 0 else total + pv
        if t < 3:
            continue
        totals.append(total)
        if h < HEADS - 1:
            continue
        finish(r, totals, [top_s[g : g + 1, :] for g in range(HEADS)])
        mass = jnp.concatenate([total[WIDTH : WIDTH + 1] for total in totals], axis=0)
        inside = jnp.logical_and(mass > LOW, mass < HIGH)
        fine.append(jnp.min(inside.astype(F32)) > 0.5)
        totals = []

    for r in range(STEP):

        @pl.when(jnp.logical_not(fine[r]))
        def _():
            totals, shifts = [], []
            for h in range(HEADS):

                def tile(t, carry):
                    largest, total = carry
                    at = pl.ds(pl.multiple_of(t * BLOCK, BLOCK), BLOCK)
                    s = matmul(k_s[r, at, :], q_s[r, h]) + bias_s[t, h].astype(F32)
                    fresh = jnp.maximum(largest, jnp.max(s, axis=0, keepdims=True))
                    p = jnp.exp2((s - fresh) * LOG2E).astype(BF16)
                    scale = jnp.exp2((largest - fresh) * LOG2E)
                    return fresh, total * scale + matmul(v_s[r, h, :, at], p)

                begin = jnp.full((1, COLS), -jnp.inf, F32), jnp.zeros((PAD, COLS), F32)
                largest, total = lax.fori_loop(0, 4, tile, begin)
                totals.append(total)
                shifts.append(largest)
            finish(r, totals, shifts)


def attend(x_q, x_ks, w_project, biases, dtype):
    def rows(x):
        return pl.BlockSpec((STEP,) + x.shape[1:], lambda i: (i, 0, 0))

    scores = ROWS * HEADS * COLS * KEYS
    return pl.pallas_call(
        functools.partial(attend_kernel, len(x_ks)),
        grid=(ROWS // STEP,),
        in_specs=[rows(x_q)]
        + [rows(x) for x in x_ks]
        + [pl.BlockSpec((CHANNELS, 512), lambda i: (0, 0))]
        + [pl.BlockSpec(memory_space=pl.ANY)] * len(biases),
        out_specs=pl.BlockSpec((STEP, PARTIAL, COLS), lambda i: (i, 0, 0)),
        out_shape=jax.ShapeDtypeStruct((ROWS, PARTIAL, COLS), dtype),
        scratch_shapes=[
            pltpu.VMEM((4, HEADS, BLOCK, COLS), BF16),
            pltpu.VMEM((HEADS, COLS), F32),
            pltpu.VMEM((STEP, KEYS, CHANNELS), BF16),
            pltpu.VMEM((STEP, HEADS, PAD, KEYS), BF16),
            pltpu.VMEM((STEP, HEADS, CHANNELS, COLS), BF16),
            pltpu.SemaphoreType.DMA((8,)),
        ],
        compiler_params=pltpu.CompilerParams(vmem_limit_bytes=VMEM_LIMIT),
        cost_estimate=pl.CostEstimate(
            flops=scores * 512, bytes_accessed=2**24, transcendentals=scores
        ),
        name="attend",
    )(x_q, *x_ks, w_project, *biases)


def update_kernel(x, w, w_out, mine, theirs, out):
    def parts(partial):
        p = partial[0].astype(F32)
        stat = p[CHANNELS : CHANNELS + 4] + p[CHANNELS + 4 : CHANNELS + 8]
        return p[:CHANNELS], stat + p[CHANNELS + 8 : CHANNELS + 12]

    (o1, stat1), (o2, stat2) = parts(mine), parts(theirs)
    share = jax.nn.sigmoid(stat1 - stat2)
    lines = [jnp.broadcast_to(share[h : h + 1], (WIDTH, COLS)) for h in range(HEADS)]
    attended = o2 + jnp.concatenate(lines, axis=0) * (o1 - o2)
    gate = jax.nn.sigmoid(matmul(w[:, 384:], x[0], 0, 1))
    gated = (gate * attended).astype(BF16)
    update = matmul(gated, w_out[...], 0, 0).astype(BF16)
    out[:, 0] = update.reshape(16, SHARE, CHANNELS)


def update_rows(x, w_project, w_out, mine, theirs):
    def row(a):
        return pl.BlockSpec((1,) + a.shape[1:], lambda i: (i, 0, 0))

    def whole(a):
        return pl.BlockSpec(a.shape, lambda i: (0, 0))

    return pl.pallas_call(
        update_kernel,
        grid=(ROWS,),
        in_specs=[row(x), whole(w_project), whole(w_out), row(mine), row(theirs)],
        out_specs=pl.BlockSpec((16, 1, SHARE, CHANNELS), lambda i: (0, i, 0, 0)),
        out_shape=jax.ShapeDtypeStruct((16, ROWS, SHARE, CHANNELS), BF16),
        compiler_params=pltpu.CompilerParams(vmem_limit_bytes=VMEM_LIMIT),
        name="update",
    )(x, w_project, w_out, mine, theirs)


def tied(x, *before):
    for array in before:
        x = x + 0 * array[(0,) * array.ndim]
    return x


def shift(x, axis, step):
    return lax.ppermute(x, axis, [(i, (i + step) % 4) for i in range(4)])


def gather_direct(x, axis):
    far = shift(x, axis, 2)
    return x, shift(x, axis, -1), far, shift(x, axis, 1)


def shards(pair_block, norm_gain, w_project, w_out, head_bias):
    own, bias_t = prepare(pair_block, norm_gain, head_bias)
    biases = [lax.all_gather(bias_t, ("y", "core"), axis=0, tiled=False)]

    xh, xl = lax.axis_index("xh"), lax.axis_index("xl")

    def send(x, *pairs):
        return lax.ppermute(x, ("xh", "xl"), pairs)

    far, across = send(own, (2, 0), (1, 3)), send(own, (1, 2), (2, 1))
    their_k = jnp.where(xl == xh, far, across)
    their_ks = gather_direct(their_k, "z")
    again = tied(own, their_k)
    their_q = jnp.where(xl == xh, far, send(again, (3, 1), (0, 2)))
    own_k = jnp.where(xl == xh, own, send(again, (0, 1), (3, 2)))
    own_ks = gather_direct(tied(own_k, *their_ks[1:]), "z")

    theirs = attend(their_q, their_ks, w_project, biases, BF16)
    theirs = lax.ppermute(theirs, "xh", [(0, 1), (1, 0)])
    mine = attend(own, own_ks, w_project, biases, F32)
    update = update_rows(own, w_project, w_out, mine, theirs)
    update = lax.all_to_all(update, ROW_AXES, split_axis=0, concat_axis=0, tiled=True)
    return jnp.transpose(update, (2, 0, 1, 3)).reshape(SHARE, 16 * ROWS, CHANNELS)


def solution(mesh):
    fine = Mesh(mesh.devices.reshape(4, 2, 2, 4, 2), ROW_AXES + COL_AXES)
    in_specs = (P(ROW_AXES, COL_AXES, None), P(), P(), P(), P(None, COL_AXES, ROW_AXES))
    out_specs = P(COL_AXES + ROW_AXES, None, None)
    return jax.shard_map(
        shards, mesh=fine, in_specs=in_specs, out_specs=out_specs, check_vma=False
    )
```

```python
import functools

import jax
import jax.numpy as jnp
from jax import lax
from jax.experimental import pallas as pl
from jax.experimental.pallas import tpu as pltpu
from jax.sharding import Mesh, PartitionSpec as P

F32, BF16 = jnp.float32, jnp.bfloat16
HEADS, WIDTH, CHANNELS = 4, 32, 128
COLS, BLOCK, ROWS = 512, 512, 4
KEYS = 4 * BLOCK
SHARE = COLS // 16
PAD = 40
PARTIAL = CHANNELS + 4 * HEADS
STEP = 2
LOG2E = 1.4426950408889634
LOW, HIGH = 1e-26, 1e30
ROW_AXES = ("y", "xh", "core")
COL_AXES = ("z", "xl")
VMEM_LIMIT = 32 * 2**20


def matmul(a, b, first=1, second=0):
    dims = (((first,), (second,)), ((), ()))
    return lax.dot_general(a, b, dims, preferred_element_type=F32)


def prepare_kernel(pair, gain, bias, normed, bias_t):
    keys = bias.shape[2]
    places = [lax.broadcasted_iota(jnp.int32, (keys, keys), axis) for axis in (0, 1)]
    identity = (places[0] == places[1]).astype(F32).astype(BF16)
    values = pair[...].astype(F32)
    centered = values - jnp.mean(values, axis=-1, keepdims=True)
    variance = jnp.mean(centered * centered, axis=-1, keepdims=True)
    normed[...] = (centered * lax.rsqrt(variance + 1e-05) * gain[...]).astype(BF16)
    for h in range(bias.shape[0]):
        bias_t[h] = matmul(identity, bias[h], 1, 1).astype(BF16)


def prepare(pair_block, norm_gain, head_bias):
    def whole(*shape):
        return pl.BlockSpec((2,) + shape, lambda i: (i, 0, 0))

    keys = head_bias.shape[2]
    return pl.pallas_call(
        prepare_kernel,
        grid=(ROWS // 2,),
        in_specs=[
            whole(COLS, CHANNELS),
            pl.BlockSpec((1, CHANNELS), lambda i: (0, 0)),
            whole(COLS, keys),
        ],
        out_specs=[whole(COLS, CHANNELS), whole(keys, COLS)],
        out_shape=[
            jax.ShapeDtypeStruct((ROWS, COLS, CHANNELS), BF16),
            jax.ShapeDtypeStruct((HEADS, keys, COLS), BF16),
        ],
        name="prepare",
    )(pair_block, norm_gain.reshape(1, CHANNELS), head_bias)


def attend_kernel(blocks, xq, *rest):
    xks, w, rest = rest[:blocks], rest[blocks], rest[blocks + 1 :]
    biases, out, (bias_s, top_s, k_s, v_s, q_s, sems) = rest[:10], rest[10], rest[11:]
    step = pl.program_id(0)
    y, z, core = lax.axis_index("y"), lax.axis_index("z"), lax.axis_index("core")

    def bias_copies():
        copies = []
        for n, ref in enumerate(biases):
            place = (0, 1, 3, 2, 2)[n // 2]
            heads = pl.ds((0, 0, 0, 0, 2)[n // 2], ref.shape[0])
            slot = lax.rem(y - z + 4 + place, 4)
            half = core if n % 2 == 0 else 1 - core
            at = pl.ds(pl.multiple_of(half * 256, 256), 256)
            copies.append(pltpu.make_async_copy(ref, bias_s.at[slot, heads, at, :], sems.at[n]))
        return copies

    @pl.when(step == 0)
    def _():
        for copy in bias_copies():
            copy.start()
        q_s[...] = jnp.zeros_like(q_s)
        v_s[:, :, WIDTH:, :] = jnp.ones((STEP, HEADS, PAD - WIDTH, KEYS), BF16)

    def project(r):
        x_q = xq[r]
        q_t = (matmul(w[:, :128], x_q, 0, 1) * WIDTH ** (-0.5)).astype(BF16)
        for h in range(HEADS):
            at = slice(h * WIDTH, (h + 1) * WIDTH)
            q_s[r, h, at, :] = q_t[at]
        start = 0
        for x in xks:
            size = x.shape[1]
            at = slice(start, start + size)
            k_s[r, at, :] = matmul(x[r], w[:, 128:256]).astype(BF16)
            v_t = matmul(w[:, 256:384], x[r], 0, 1).astype(BF16)
            for h in range(HEADS):
                v_s[r, h, :WIDTH, at] = v_t[h * WIDTH : (h + 1) * WIDTH]
            start += size

    def finish(r, totals, shifts):
        parts, stats = [], []
        for total, shift in zip(totals, shifts):
            mass = total[WIDTH : WIDTH + 1]
            parts.append(total[:WIDTH] * (1.0 / mass))
            stats.append(shift + jnp.log(mass))
        stat = jnp.concatenate(stats, axis=0)
        high = stat.astype(BF16).astype(F32)
        middle = (stat - high).astype(BF16).astype(F32)
        low = stat - high - middle
        rows = parts + [high, middle, low, jnp.zeros_like(low)]
        out[r] = jnp.concatenate(rows, axis=0).astype(out.dtype)

    for r in range(STEP):
        project(r)

    @pl.when(step == 0)
    def _():
        for copy in bias_copies():
            copy.wait()
        for h in range(HEADS):
            tops = [jnp.max(bias_s[t, h], axis=0, keepdims=True) for t in range(4)]
            top = jnp.maximum(jnp.maximum(tops[0], tops[1]), jnp.maximum(tops[2], tops[3]))
            top_s[h : h + 1, :] = top.astype(F32)

    units = [(r, h, t) for r in range(STEP) for h in range(HEADS) for t in range(4)]

    def scores(r, h, t):
        at = slice(t * BLOCK, (t + 1) * BLOCK)
        return matmul(k_s[r, at, :], q_s[r, h]) + bias_s[t, h].astype(F32)

    fine, totals = [], []
    ahead, total = scores(*units[0]), None
    for n, (r, h, t) in enumerate(units):
        s, shift = ahead, top_s[h : h + 1, :]
        if n + 1 < len(units):
            ahead = scores(*units[n + 1])
        p = jnp.exp2((s - shift) * LOG2E).astype(BF16)
        pv = matmul(v_s[r, h, :, t * BLOCK : (t + 1) * BLOCK], p)
        total = pv if t == 0 else total + pv
        if t < 3:
            continue
        totals.append(total)
        if h < HEADS - 1:
            continue
        finish(r, totals, [top_s[g : g + 1, :] for g in range(HEADS)])
        mass = jnp.concatenate([total[WIDTH : WIDTH + 1] for total in totals], axis=0)
        inside = jnp.logical_and(mass > LOW, mass < HIGH)
        fine.append(jnp.min(inside.astype(F32)) > 0.5)
        totals = []

    for r in range(STEP):

        @pl.when(jnp.logical_not(fine[r]))
        def _():
            totals, shifts = [], []
            for h in range(HEADS):

                def tile(t, carry):
                    largest, total = carry
                    at = pl.ds(pl.multiple_of(t * BLOCK, BLOCK), BLOCK)
                    s = matmul(k_s[r, at, :], q_s[r, h]) + bias_s[t, h].astype(F32)
                    fresh = jnp.maximum(largest, jnp.max(s, axis=0, keepdims=True))
                    p = jnp.exp2((s - fresh) * LOG2E).astype(BF16)
                    scale = jnp.exp2((largest - fresh) * LOG2E)
                    return fresh, total * scale + matmul(v_s[r, h, :, at], p)

                begin = jnp.full((1, COLS), -jnp.inf, F32), jnp.zeros((PAD, COLS), F32)
                largest, total = lax.fori_loop(0, 4, tile, begin)
                totals.append(total)
                shifts.append(largest)
            finish(r, totals, shifts)


def attend(x_q, x_ks, w_project, biases, dtype):
    def rows(x):
        return pl.BlockSpec((STEP,) + x.shape[1:], lambda i: (i, 0, 0))

    scores = ROWS * HEADS * COLS * KEYS
    return pl.pallas_call(
        functools.partial(attend_kernel, len(x_ks)),
        grid=(ROWS // STEP,),
        in_specs=[rows(x_q)]
        + [rows(x) for x in x_ks]
        + [pl.BlockSpec((CHANNELS, 512), lambda i: (0, 0))]
        + [pl.BlockSpec(memory_space=pl.ANY)] * len(biases),
        out_specs=pl.BlockSpec((STEP, PARTIAL, COLS), lambda i: (i, 0, 0)),
        out_shape=jax.ShapeDtypeStruct((ROWS, PARTIAL, COLS), dtype),
        scratch_shapes=[
            pltpu.VMEM((4, HEADS, BLOCK, COLS), BF16),
            pltpu.VMEM((HEADS, COLS), F32),
            pltpu.VMEM((STEP, KEYS, CHANNELS), BF16),
            pltpu.VMEM((STEP, HEADS, PAD, KEYS), BF16),
            pltpu.VMEM((STEP, HEADS, CHANNELS, COLS), BF16),
            pltpu.SemaphoreType.DMA((10,)),
        ],
        compiler_params=pltpu.CompilerParams(vmem_limit_bytes=VMEM_LIMIT),
        cost_estimate=pl.CostEstimate(
            flops=scores * 512, bytes_accessed=2**24, transcendentals=scores
        ),
        name="attend",
    )(x_q, *x_ks, w_project, *biases)


def update_kernel(x, w, w_out, mine, theirs, out):
    def parts(partial):
        p = partial[0].astype(F32)
        stat = p[CHANNELS : CHANNELS + 4] + p[CHANNELS + 4 : CHANNELS + 8]
        return p[:CHANNELS], stat + p[CHANNELS + 8 : CHANNELS + 12]

    (o1, stat1), (o2, stat2) = parts(mine), parts(theirs)
    share = jax.nn.sigmoid(stat1 - stat2)
    lines = [jnp.broadcast_to(share[h : h + 1], (WIDTH, COLS)) for h in range(HEADS)]
    attended = o2 + jnp.concatenate(lines, axis=0) * (o1 - o2)
    gate = jax.nn.sigmoid(matmul(w[:, 384:], x[0], 0, 1))
    gated = (gate * attended).astype(BF16)
    update = matmul(gated, w_out[...], 0, 0).astype(BF16)
    out[:, 0] = update.reshape(16, SHARE, CHANNELS)


def update_rows(x, w_project, w_out, mine, theirs):
    def row(a):
        return pl.BlockSpec((1,) + a.shape[1:], lambda i: (i, 0, 0))

    def whole(a):
        return pl.BlockSpec(a.shape, lambda i: (0, 0))

    return pl.pallas_call(
        update_kernel,
        grid=(ROWS,),
        in_specs=[row(x), whole(w_project), whole(w_out), row(mine), row(theirs)],
        out_specs=pl.BlockSpec((16, 1, SHARE, CHANNELS), lambda i: (0, i, 0, 0)),
        out_shape=jax.ShapeDtypeStruct((16, ROWS, SHARE, CHANNELS), BF16),
        compiler_params=pltpu.CompilerParams(vmem_limit_bytes=VMEM_LIMIT),
        name="update",
    )(x, w_project, w_out, mine, theirs)


def tied(x, *before):
    for array in before:
        x = x + 0 * array[(0,) * array.ndim]
    return x


def shift(x, axis, step):
    return lax.ppermute(x, axis, [(i, (i + step) % 4) for i in range(4)])


def swap(x):
    return lax.ppermute(x, "core", [(0, 1), (1, 0)])


def gather_direct(x, axis):
    far = shift(x, axis, 2)
    return x, shift(x, axis, -1), far, shift(x, axis, 1)


def shards(pair_block, norm_gain, w_project, w_out, head_bias):
    own, bias_t = prepare(pair_block, norm_gain, head_bias)
    bias_own = bias_t, swap(bias_t)
    behind, ahead = shift(bias_t, "y", 1), shift(bias_t, "y", -1)

    xh, xl = lax.axis_index("xh"), lax.axis_index("xl")

    def send(x, *pairs):
        return lax.ppermute(x, ("xh", "xl"), pairs)

    far, across = send(own, (2, 0), (1, 3)), send(own, (1, 2), (2, 1))
    their_k = tied(jnp.where(xl == xh, far, across), bias_own[1])
    their_ks = gather_direct(their_k, "z")
    again = tied(own, their_k)
    their_q = jnp.where(xl == xh, far, send(again, (3, 1), (0, 2)))
    own_k = jnp.where(xl == xh, own, send(again, (0, 1), (3, 2)))
    own_ks = gather_direct(tied(own_k, *their_ks[1:]), "z")

    far = shift(tied(behind[:2], their_k), "y", 1), shift(tied(ahead[2:], their_k), "y", -1)
    biases = [*bias_own]
    for block in (ahead, behind, *far):
        biases += [block, swap(block)]

    theirs = attend(their_q, their_ks, w_project, biases, BF16)
    theirs = lax.ppermute(theirs, "xh", [(0, 1), (1, 0)])
    mine = attend(own, own_ks, w_project, biases, F32)
    update = update_rows(own, w_project, w_out, mine, theirs)
    update = lax.all_to_all(update, ROW_AXES, split_axis=0, concat_axis=0, tiled=True)
    return jnp.transpose(update, (2, 0, 1, 3)).reshape(SHARE, 16 * ROWS, CHANNELS)


def solution(mesh):
    fine = Mesh(mesh.devices.reshape(4, 2, 2, 4, 2), ROW_AXES + COL_AXES)
    in_specs = (P(ROW_AXES, COL_AXES, None), P(), P(), P(), P(None, COL_AXES, ROW_AXES))
    out_specs = P(COL_AXES + ROW_AXES, None, None)
    return jax.shard_map(
        shards, mesh=fine, in_specs=in_specs, out_specs=out_specs, check_vma=False
    )
```

```python
import functools

import jax
import jax.numpy as jnp
from jax import lax
from jax.experimental import pallas as pl
from jax.experimental.pallas import tpu as pltpu
from jax.sharding import Mesh, PartitionSpec as P

F32, BF16 = jnp.float32, jnp.bfloat16
HEADS, WIDTH, CHANNELS = 4, 32, 128
COLS, BLOCK, ROWS = 512, 512, 4
KEYS = 4 * BLOCK
SHARE = COLS // 16
PAD = 40
STEP = 2
LOG2E = 1.4426950408889634
LOW, HIGH = 1e-26, 1e30
ROW_AXES = ("y", "xh", "core")
COL_AXES = ("z", "xl")
VMEM_LIMIT = 32 * 2**20


def matmul(a, b, first=1, second=0):
    dims = (((first,), (second,)), ((), ()))
    return lax.dot_general(a, b, dims, preferred_element_type=F32)


def prepare_kernel(pair, gain, bias, normed, bias_t):
    keys = bias.shape[2]
    places = [lax.broadcasted_iota(jnp.int32, (keys, keys), axis) for axis in (0, 1)]
    identity = (places[0] == places[1]).astype(F32).astype(BF16)
    values = pair[...].astype(F32)
    centered = values - jnp.mean(values, axis=-1, keepdims=True)
    variance = jnp.mean(centered * centered, axis=-1, keepdims=True)
    normed[...] = (centered * lax.rsqrt(variance + 1e-05) * gain[...]).astype(BF16)
    for h in range(bias.shape[0]):
        bias_t[h] = matmul(identity, bias[h], 1, 1).astype(BF16)


def prepare(pair_block, norm_gain, head_bias):
    def whole(*shape):
        return pl.BlockSpec((2,) + shape, lambda i: (i, 0, 0))

    keys = head_bias.shape[2]
    return pl.pallas_call(
        prepare_kernel,
        grid=(ROWS // 2,),
        in_specs=[
            whole(COLS, CHANNELS),
            pl.BlockSpec((1, CHANNELS), lambda i: (0, 0)),
            whole(COLS, keys),
        ],
        out_specs=[whole(COLS, CHANNELS), whole(keys, COLS)],
        out_shape=[
            jax.ShapeDtypeStruct((ROWS, COLS, CHANNELS), BF16),
            jax.ShapeDtypeStruct((HEADS, keys, COLS), BF16),
        ],
        name="prepare",
    )(pair_block, norm_gain.reshape(1, CHANNELS), head_bias)


def attend_kernel(blocks, xq, *rest):
    xks, w, rest = rest[:blocks], rest[blocks], rest[blocks + 1 :]
    biases, out, scratch = rest[:10], rest[-9], rest[-8:]
    bias_s, top_s, k_s, v_s, q_s, gate_s, stat_s, sems = scratch
    step = pl.program_id(0)

    y, z, core = lax.axis_index("y"), lax.axis_index("z"), lax.axis_index("core")

    def bias_copies():
        copies = []
        for n, ref in enumerate(biases):
            place = (0, 1, 3, 2, 2)[n // 2]
            heads = pl.ds((0, 0, 0, 0, 2)[n // 2], ref.shape[0])
            slot = lax.rem(y - z + 4 + place, 4)
            half = core if n % 2 == 0 else 1 - core
            at = pl.ds(pl.multiple_of(half * 256, 256), 256)
            copies.append(pltpu.make_async_copy(ref, bias_s.at[slot, heads, at, :], sems.at[n]))
        return copies

    @pl.when(step == 0)
    def _():
        for copy in bias_copies():
            copy.start()
        q_s[...] = jnp.zeros_like(q_s)
        stat_s[...] = jnp.zeros_like(stat_s)
        v_s[:, :, WIDTH:, :] = jnp.ones((STEP, HEADS, PAD - WIDTH, KEYS), BF16)

    def project(r):
        x_q = xq[r]
        q_t = (matmul(w[:, :128], x_q, 0, 1) * WIDTH ** (-0.5)).astype(BF16)
        gate_s[r] = jax.nn.sigmoid(matmul(w[:, 384:], x_q, 0, 1))
        for h in range(HEADS):
            at = slice(h * WIDTH, (h + 1) * WIDTH)
            q_s[r, h, at, :] = q_t[at]
        start = 0
        for x in xks:
            size = x.shape[1]
            at = slice(start, start + size)
            k_s[r, at, :] = matmul(x[r], w[:, 128:256]).astype(BF16)
            v_t = matmul(w[:, 256:384], x[r], 0, 1).astype(BF16)
            for h in range(HEADS):
                v_s[r, h, :WIDTH, at] = v_t[h * WIDTH : (h + 1) * WIDTH]
            start += size

    def finish(r, totals, shifts):
        parts, stats = [], []
        for total, shift in zip(totals, shifts):
            mass = total[WIDTH : WIDTH + 1]
            parts.append(total[:WIDTH] * (1.0 / mass))
            stats.append(shift + jnp.log(mass))
        gated = jnp.concatenate(parts, axis=0) * gate_s[r]
        at = step * STEP + r
        out[:, at] = gated.T.astype(BF16).reshape(16, SHARE, CHANNELS)
        stat = jnp.concatenate(stats, axis=0)
        high = stat.astype(BF16).astype(F32)
        middle = (stat - high).astype(BF16).astype(F32)
        low = stat - high - middle
        rows = jnp.concatenate([high, middle, low, jnp.zeros_like(low)], axis=0)
        stat_s[pl.ds(pl.multiple_of(at * 32, 32), 16), :] = rows

    for r in range(STEP):
        project(r)

    @pl.when(step == 0)
    def _():
        for copy in bias_copies():
            copy.wait()
        for h in range(HEADS):
            tops = [jnp.max(bias_s[t, h], axis=0, keepdims=True) for t in range(4)]
            top = jnp.maximum(jnp.maximum(tops[0], tops[1]), jnp.maximum(tops[2], tops[3]))
            top_s[h : h + 1, :] = top.astype(F32)

    units = [(r, h, t) for r in range(STEP) for h in range(HEADS) for t in range(4)]

    def scores(r, h, t):
        at = slice(t * BLOCK, (t + 1) * BLOCK)
        return matmul(k_s[r, at, :], q_s[r, h]) + bias_s[t, h].astype(F32)

    fine, totals = [], []
    ahead, total = scores(*units[0]), None
    for n, (r, h, t) in enumerate(units):
        s, shift = ahead, top_s[h : h + 1, :]
        if n + 1 < len(units):
            ahead = scores(*units[n + 1])
        p = jnp.exp2((s - shift) * LOG2E).astype(BF16)
        pv = matmul(v_s[r, h, :, t * BLOCK : (t + 1) * BLOCK], p)
        total = pv if t == 0 else total + pv
        if t < 3:
            continue
        totals.append(total)
        if h < HEADS - 1:
            continue
        finish(r, totals, [top_s[g : g + 1, :] for g in range(HEADS)])
        mass = jnp.concatenate([total[WIDTH : WIDTH + 1] for total in totals], axis=0)
        inside = jnp.logical_and(mass > LOW, mass < HIGH)
        fine.append(jnp.min(inside.astype(F32)) > 0.5)
        totals = []

    for r in range(STEP):

        @pl.when(jnp.logical_not(fine[r]))
        def _():
            totals, shifts = [], []
            for h in range(HEADS):

                def tile(t, carry):
                    largest, total = carry
                    at = pl.ds(pl.multiple_of(t * BLOCK, BLOCK), BLOCK)
                    s = matmul(k_s[r, at, :], q_s[r, h]) + bias_s[t, h].astype(F32)
                    fresh = jnp.maximum(largest, jnp.max(s, axis=0, keepdims=True))
                    p = jnp.exp2((s - fresh) * LOG2E).astype(BF16)
                    scale = jnp.exp2((largest - fresh) * LOG2E)
                    return fresh, total * scale + matmul(v_s[r, h, :, at], p)

                begin = jnp.full((1, COLS), -jnp.inf, F32), jnp.zeros((PAD, COLS), F32)
                largest, total = lax.fori_loop(0, 4, tile, begin)
                totals.append(total)
                shifts.append(largest)
            finish(r, totals, shifts)

    @pl.when(step == pl.num_programs(0) - 1)
    def _():
        out[:, ROWS] = stat_s[...].T.astype(BF16).reshape(16, SHARE, CHANNELS)


def attend(x_q, x_ks, w_project, biases, message=()):
    half = len(message)

    def rows(x):
        return pl.BlockSpec((STEP,) + x.shape[1:], lambda i: (i, 0, 0))

    scores = ROWS * HEADS * COLS * KEYS
    block = (16, ROWS + 1, SHARE, CHANNELS)
    return pl.pallas_call(
        functools.partial(attend_kernel, len(x_ks)),
        grid=(ROWS // STEP,),
        in_specs=[rows(x_q)]
        + [rows(x) for x in x_ks]
        + [pl.BlockSpec((CHANNELS, 512), lambda i: (0, 0))]
        + [pl.BlockSpec(memory_space=pl.ANY)] * (len(biases) + len(message)),
        out_specs=pl.BlockSpec(block, lambda i: (0, half, 0, 0)),
        out_shape=jax.ShapeDtypeStruct((16, 2 * (ROWS + 1), SHARE, CHANNELS), BF16),
        input_output_aliases={2 + len(x_ks) + len(biases): 0} if half else {},
        scratch_shapes=[
            pltpu.VMEM((4, HEADS, BLOCK, COLS), BF16),
            pltpu.VMEM((HEADS, COLS), F32),
            pltpu.VMEM((STEP, KEYS, CHANNELS), BF16),
            pltpu.VMEM((STEP, HEADS, PAD, KEYS), BF16),
            pltpu.VMEM((STEP, HEADS, CHANNELS, COLS), BF16),
            pltpu.VMEM((STEP, CHANNELS, COLS), F32),
            pltpu.VMEM((CHANNELS, COLS), F32),
            pltpu.SemaphoreType.DMA((10,)),
        ],
        compiler_params=pltpu.CompilerParams(vmem_limit_bytes=VMEM_LIMIT),
        cost_estimate=pl.CostEstimate(
            flops=scores * 512, bytes_accessed=2**24, transcendentals=scores
        ),
        name="attend",
    )(x_q, *x_ks, w_project, *biases, *message)


def merge_kernel(message, w, out):
    lane = lax.broadcasted_iota(jnp.int32, (CHANNELS, CHANNELS), 0)
    head = lax.broadcasted_iota(jnp.int32, (CHANNELS, CHANNELS), 1) // WIDTH
    rows = []
    for s in range(4):
        other = s ^ 2
        stat1, stat2 = message[s, ROWS], message[other, 2 * ROWS + 1]
        for i in range(ROWS):
            part = lane - 32 * i
            inside = (part >= 0) & (part < 12) & (lax.rem(part, 4) == head)
            pick = inside.astype(F32).astype(BF16)
            share = jax.nn.sigmoid(matmul(stat1, pick) - matmul(stat2, pick))
            o1 = message[s, i].astype(F32)
            o2 = message[other, ROWS + 1 + i].astype(F32)
            rows.append((o2 + share * (o1 - o2)).astype(BF16))
    update = matmul(jnp.concatenate(rows, axis=0), w[...])
    update = jnp.swapaxes(update.reshape(4 * ROWS, SHARE, CHANNELS), 0, 1)
    out[...] = update.astype(BF16)


def merge(message, w_out):
    return pl.pallas_call(
        merge_kernel,
        grid=(4,),
        in_specs=[
            pl.BlockSpec((4,) + message.shape[1:], lambda y: (y, 0, 0, 0)),
            pl.BlockSpec((CHANNELS, CHANNELS), lambda y: (0, 0)),
        ],
        out_specs=pl.BlockSpec((SHARE, 4 * ROWS, CHANNELS), lambda y: (0, y, 0)),
        out_shape=jax.ShapeDtypeStruct((SHARE, 16 * ROWS, CHANNELS), BF16),
        compiler_params=pltpu.CompilerParams(vmem_limit_bytes=VMEM_LIMIT),
        name="merge",
    )(message, w_out)


def tied(x, *before):
    for array in before:
        x = x + 0 * array[(0,) * array.ndim]
    return x


def shift(x, axis, step):
    return lax.ppermute(x, axis, [(i, (i + step) % 4) for i in range(4)])


def swap(x):
    return lax.ppermute(x, "core", [(0, 1), (1, 0)])


def gather_direct(x, axis):
    return x, shift(x, axis, -1), shift(x, axis, 2), shift(x, axis, 1)


def gather_ring(x, axis):
    behind, ahead = shift(x, axis, 1), shift(x, axis, -1)
    parts = tied(behind[:, :256], ahead), tied(ahead[:, 256:], behind)
    far = shift(parts[0], axis, 1), shift(parts[1], axis, -1)
    return x, ahead, *far, behind


def gather_bias(block):
    behind, ahead = shift(block, "y", 1), shift(block, "y", -1)
    far = [shift(behind[:2], "y", 1), shift(ahead[2:], "y", -1)]
    return [side for b in (block, ahead, behind, *far) for side in (b, swap(b))]


def shards(pair_block, norm_gain, w_project, w_out, head_bias):
    own, bias_t = prepare(pair_block, norm_gain, head_bias)
    biases = gather_bias(bias_t)

    xh, xl = lax.axis_index("xh"), lax.axis_index("xl")
    behind, ahead = shift(own, ("xh", "xl"), 1), shift(own, ("xh", "xl"), -1)
    opposite = shift(behind, ("xh", "xl"), 1)
    near = jnp.where(xh == 0, behind, ahead)
    first_ks = gather_ring(tied(jnp.where(xl == xh, own, near), biases[1]), "z")
    near = jnp.where(xh == 0, ahead, behind)
    second_ks = gather_direct(tied(jnp.where(xl == xh, opposite, near), first_ks[1], first_ks[4]), "z")

    message = attend(own, first_ks, w_project, biases)
    message = attend(opposite, second_ks, w_project, biases, (message,))
    message = lax.all_to_all(message, ROW_AXES, split_axis=0, concat_axis=0, tiled=True)
    return merge(message, w_out)


def solution(mesh):
    fine = Mesh(mesh.devices.reshape(4, 2, 2, 4, 2), ROW_AXES + COL_AXES)
    in_specs = (P(ROW_AXES, COL_AXES, None), P(), P(), P(), P(None, COL_AXES, ROW_AXES))
    out_specs = P(COL_AXES + ROW_AXES, None, None)
    return jax.shard_map(
        shards, mesh=fine, in_specs=in_specs, out_specs=out_specs, check_vma=False
    )
```

```python
import functools

import jax
import jax.numpy as jnp
from jax import lax
from jax.experimental import pallas as pl
from jax.experimental.pallas import tpu as pltpu
from jax.sharding import Mesh, PartitionSpec as P

F32, BF16 = jnp.float32, jnp.bfloat16
HEADS, WIDTH, CHANNELS = 4, 32, 128
COLS, BLOCK, ROWS = 512, 512, 4
KEYS = 4 * BLOCK
SHARE = COLS // 16
PAD = 40
STEP = 2
LOG2E = 1.4426950408889634
LOW, HIGH = 1e-26, 1e30
ROW_AXES = ("y", "xh", "core")
COL_AXES = ("z", "xl")
VMEM_LIMIT = 40 * 2**20


def matmul(a, b, first=1, second=0):
    dims = (((first,), (second,)), ((), ()))
    return lax.dot_general(a, b, dims, preferred_element_type=F32)


def prepare_kernel(pair, gain, bias, normed, bias_t):
    keys = bias.shape[2]
    places = [lax.broadcasted_iota(jnp.int32, (keys, keys), axis) for axis in (0, 1)]
    identity = (places[0] == places[1]).astype(F32).astype(BF16)
    values = pair[...].astype(F32)
    centered = values - jnp.mean(values, axis=-1, keepdims=True)
    variance = jnp.mean(centered * centered, axis=-1, keepdims=True)
    normed[...] = (centered * lax.rsqrt(variance + 1e-05) * gain[...]).astype(BF16)
    for h in range(bias.shape[0]):
        bias_t[h] = matmul(identity, bias[h], 1, 1).astype(BF16)


def prepare(pair_block, norm_gain, head_bias):
    def whole(*shape):
        return pl.BlockSpec((2,) + shape, lambda i: (i, 0, 0))

    keys = head_bias.shape[2]
    return pl.pallas_call(
        prepare_kernel,
        grid=(ROWS // 2,),
        in_specs=[
            whole(COLS, CHANNELS),
            pl.BlockSpec((1, CHANNELS), lambda i: (0, 0)),
            whole(COLS, keys),
        ],
        out_specs=[whole(COLS, CHANNELS), whole(keys, COLS)],
        out_shape=[
            jax.ShapeDtypeStruct((ROWS, COLS, CHANNELS), BF16),
            jax.ShapeDtypeStruct((HEADS, keys, COLS), BF16),
        ],
        name="prepare",
    )(pair_block, norm_gain.reshape(1, CHANNELS), head_bias)


def attend_kernel(blocks, xq, *rest):
    xks, w, rest = rest[:blocks], rest[blocks], rest[blocks + 1 :]
    biases, out, scratch = rest[:10], rest[-10], rest[-9:]
    bias_s, scaled_s, top_s, k_s, v_s, q_s, gate_s, stat_s, sems = scratch
    step = pl.program_id(0)

    y, z, core = lax.axis_index("y"), lax.axis_index("z"), lax.axis_index("core")

    def bias_copies():
        copies = []
        for n, ref in enumerate(biases):
            place = (0, 1, 3, 2, 2)[n // 2]
            heads = pl.ds((0, 0, 0, 0, 2)[n // 2], ref.shape[0])
            slot = lax.rem(y - z + 4 + place, 4)
            half = core if n % 2 == 0 else 1 - core
            at = pl.ds(pl.multiple_of(half * 256, 256), 256)
            copies.append(pltpu.make_async_copy(ref, bias_s.at[slot, heads, at, :], sems.at[n]))
        return copies

    @pl.when(step == 0)
    def _():
        for copy in bias_copies():
            copy.start()
        q_s[...] = jnp.zeros_like(q_s)
        stat_s[...] = jnp.zeros_like(stat_s)
        v_s[:, :, WIDTH:, :] = jnp.ones((STEP, HEADS, PAD - WIDTH, KEYS), BF16)

    def project(r):
        x_q = xq[r]
        q_t = (matmul(w[:, :128], x_q, 0, 1) * WIDTH ** (-0.5)).astype(BF16)
        gate_s[r] = jax.nn.sigmoid(matmul(w[:, 384:], x_q, 0, 1))
        for h in range(HEADS):
            at = slice(h * WIDTH, (h + 1) * WIDTH)
            q_s[r, h, at, :] = q_t[at]
        start = 0
        for x in xks:
            size = x.shape[1]
            at = slice(start, start + size)
            k_s[r, at, :] = matmul(x[r], w[:, 128:256]).astype(BF16)
            v_t = matmul(w[:, 256:384], x[r], 0, 1).astype(BF16)
            for h in range(HEADS):
                v_s[r, h, :WIDTH, at] = v_t[h * WIDTH : (h + 1) * WIDTH]
            start += size

    def finish(r, totals, shifts):
        parts, stats = [], []
        for total, shift in zip(totals, shifts):
            mass = total[WIDTH : WIDTH + 1]
            parts.append(total[:WIDTH] * (1.0 / mass))
            stats.append(shift + jnp.log(mass))
        gated = jnp.concatenate(parts, axis=0) * gate_s[r]
        at = step * STEP + r
        out[:, at] = gated.T.astype(BF16).reshape(16, SHARE, CHANNELS)
        stat = jnp.concatenate(stats, axis=0)
        high = stat.astype(BF16).astype(F32)
        middle = (stat - high).astype(BF16).astype(F32)
        low = stat - high - middle
        rows = jnp.concatenate([high, middle, low, jnp.zeros_like(low)], axis=0)
        stat_s[pl.ds(pl.multiple_of(at * 32, 32), 16), :] = rows

    for r in range(STEP):
        project(r)

    @pl.when(step == 0)
    def _():
        for copy in bias_copies():
            copy.wait()
        for h in range(HEADS):
            tops = [jnp.max(bias_s[t, h], axis=0, keepdims=True) for t in range(4)]
            top = jnp.maximum(jnp.maximum(tops[0], tops[1]), jnp.maximum(tops[2], tops[3]))
            top = top.astype(F32)
            top_s[h : h + 1, :] = top
            for t in range(4):
                scaled_s[t, h] = (bias_s[t, h].astype(F32) - top) * LOG2E

    units = [(r, h, t) for r in range(STEP) for h in range(HEADS) for t in range(4)]

    def scores(r, h, t):
        at = slice(t * BLOCK, (t + 1) * BLOCK)
        return matmul(k_s[r, at, :], q_s[r, h])

    fine, totals = [], []
    ahead, total = scores(*units[0]), None
    for n, (r, h, t) in enumerate(units):
        s = ahead
        if n + 1 < len(units):
            ahead = scores(*units[n + 1])
        p = jnp.exp2(s * LOG2E + scaled_s[t, h]).astype(BF16)
        pv = matmul(v_s[r, h, :, t * BLOCK : (t + 1) * BLOCK], p)
        total = pv if t == 0 else total + pv
        if t < 3:
            continue
        totals.append(total)
        if h < HEADS - 1:
            continue
        finish(r, totals, [top_s[g : g + 1, :] for g in range(HEADS)])
        mass = jnp.concatenate([total[WIDTH : WIDTH + 1] for total in totals], axis=0)
        inside = jnp.logical_and(mass > LOW, mass < HIGH)
        fine.append(jnp.min(inside.astype(F32)) > 0.5)
        totals = []

    for r in range(STEP):

        @pl.when(jnp.logical_not(fine[r]))
        def _():
            totals, shifts = [], []
            for h in range(HEADS):

                def tile(t, carry):
                    largest, total = carry
                    at = pl.ds(pl.multiple_of(t * BLOCK, BLOCK), BLOCK)
                    s = matmul(k_s[r, at, :], q_s[r, h]) + bias_s[t, h].astype(F32)
                    fresh = jnp.maximum(largest, jnp.max(s, axis=0, keepdims=True))
                    p = jnp.exp2((s - fresh) * LOG2E).astype(BF16)
                    scale = jnp.exp2((largest - fresh) * LOG2E)
                    return fresh, total * scale + matmul(v_s[r, h, :, at], p)

                begin = jnp.full((1, COLS), -jnp.inf, F32), jnp.zeros((PAD, COLS), F32)
                largest, total = lax.fori_loop(0, 4, tile, begin)
                totals.append(total)
                shifts.append(largest)
            finish(r, totals, shifts)

    @pl.when(step == pl.num_programs(0) - 1)
    def _():
        out[:, ROWS] = stat_s[...].T.astype(BF16).reshape(16, SHARE, CHANNELS)


def attend(x_q, x_ks, w_project, biases, message=()):
    half = len(message)

    def rows(x):
        return pl.BlockSpec((STEP,) + x.shape[1:], lambda i: (i, 0, 0))

    scores = ROWS * HEADS * COLS * KEYS
    block = (16, ROWS + 1, SHARE, CHANNELS)
    return pl.pallas_call(
        functools.partial(attend_kernel, len(x_ks)),
        grid=(ROWS // STEP,),
        in_specs=[rows(x_q)]
        + [rows(x) for x in x_ks]
        + [pl.BlockSpec((CHANNELS, 512), lambda i: (0, 0))]
        + [pl.BlockSpec(memory_space=pl.ANY)] * (len(biases) + len(message)),
        out_specs=pl.BlockSpec(block, lambda i: (0, half, 0, 0)),
        out_shape=jax.ShapeDtypeStruct((16, 2 * (ROWS + 1), SHARE, CHANNELS), BF16),
        input_output_aliases={2 + len(x_ks) + len(biases): 0} if half else {},
        scratch_shapes=[
            pltpu.VMEM((4, HEADS, BLOCK, COLS), BF16),
            pltpu.VMEM((4, HEADS, BLOCK, COLS), F32),
            pltpu.VMEM((HEADS, COLS), F32),
            pltpu.VMEM((STEP, KEYS, CHANNELS), BF16),
            pltpu.VMEM((STEP, HEADS, PAD, KEYS), BF16),
            pltpu.VMEM((STEP, HEADS, CHANNELS, COLS), BF16),
            pltpu.VMEM((STEP, CHANNELS, COLS), F32),
            pltpu.VMEM((CHANNELS, COLS), F32),
            pltpu.SemaphoreType.DMA((10,)),
        ],
        compiler_params=pltpu.CompilerParams(vmem_limit_bytes=VMEM_LIMIT),
        cost_estimate=pl.CostEstimate(
            flops=scores * 512, bytes_accessed=2**24, transcendentals=scores
        ),
        name="attend",
    )(x_q, *x_ks, w_project, *biases, *message)


def merge_kernel(message, w, out):
    lane = lax.broadcasted_iota(jnp.int32, (CHANNELS, CHANNELS), 0)
    head = lax.broadcasted_iota(jnp.int32, (CHANNELS, CHANNELS), 1) // WIDTH
    rows = []
    for s in range(4):
        other = s ^ 2
        stat1, stat2 = message[s, ROWS], message[other, 2 * ROWS + 1]
        for i in range(ROWS):
            part = lane - 32 * i
            inside = (part >= 0) & (part < 12) & (lax.rem(part, 4) == head)
            pick = inside.astype(F32).astype(BF16)
            share = jax.nn.sigmoid(matmul(stat1, pick) - matmul(stat2, pick))
            o1 = message[s, i].astype(F32)
            o2 = message[other, ROWS + 1 + i].astype(F32)
            rows.append((o2 + share * (o1 - o2)).astype(BF16))
    update = matmul(jnp.concatenate(rows, axis=0), w[...])
    update = jnp.swapaxes(update.reshape(4 * ROWS, SHARE, CHANNELS), 0, 1)
    out[...] = update.astype(BF16)


def merge(message, w_out):
    return pl.pallas_call(
        merge_kernel,
        grid=(4,),
        in_specs=[
            pl.BlockSpec((4,) + message.shape[1:], lambda y: (y, 0, 0, 0)),
            pl.BlockSpec((CHANNELS, CHANNELS), lambda y: (0, 0)),
        ],
        out_specs=pl.BlockSpec((SHARE, 4 * ROWS, CHANNELS), lambda y: (0, y, 0)),
        out_shape=jax.ShapeDtypeStruct((SHARE, 16 * ROWS, CHANNELS), BF16),
        compiler_params=pltpu.CompilerParams(vmem_limit_bytes=VMEM_LIMIT),
        name="merge",
    )(message, w_out)


def tied(x, *before):
    for array in before:
        x = x + 0 * array[(0,) * array.ndim]
    return x


def shift(x, axis, step):
    return lax.ppermute(x, axis, [(i, (i + step) % 4) for i in range(4)])


def swap(x):
    return lax.ppermute(x, "core", [(0, 1), (1, 0)])


def gather_direct(x, axis):
    return x, shift(x, axis, -1), shift(x, axis, 2), shift(x, axis, 1)


def gather_ring(x, axis):
    behind, ahead = shift(x, axis, 1), shift(x, axis, -1)
    parts = tied(behind[:, :256], ahead), tied(ahead[:, 256:], behind)
    far = shift(parts[0], axis, 1), shift(parts[1], axis, -1)
    return x, ahead, *far, behind


def gather_bias(block):
    behind, ahead = shift(block, "y", 1), shift(block, "y", -1)
    far = [shift(behind[:2], "y", 1), shift(ahead[2:], "y", -1)]
    return [side for b in (block, ahead, behind, *far) for side in (b, swap(b))]


def shards(pair_block, norm_gain, w_project, w_out, head_bias):
    own, bias_t = prepare(pair_block, norm_gain, head_bias)
    biases = gather_bias(bias_t)

    xh, xl = lax.axis_index("xh"), lax.axis_index("xl")
    behind, ahead = shift(own, ("xh", "xl"), 1), shift(own, ("xh", "xl"), -1)
    opposite = shift(behind, ("xh", "xl"), 1)
    near = jnp.where(xh == 0, behind, ahead)
    first_ks = gather_ring(tied(jnp.where(xl == xh, own, near), biases[1]), "z")
    near = jnp.where(xh == 0, ahead, behind)
    second_ks = gather_direct(tied(jnp.where(xl == xh, opposite, near), first_ks[1], first_ks[4]), "z")

    message = attend(own, first_ks, w_project, biases)
    message = attend(opposite, second_ks, w_project, biases, (message,))
    message = lax.all_to_all(message, ROW_AXES, split_axis=0, concat_axis=0, tiled=True)
    return merge(message, w_out)


def solution(mesh):
    fine = Mesh(mesh.devices.reshape(4, 2, 2, 4, 2), ROW_AXES + COL_AXES)
    in_specs = (P(ROW_AXES, COL_AXES, None), P(), P(), P(), P(None, COL_AXES, ROW_AXES))
    out_specs = P(COL_AXES + ROW_AXES, None, None)
    return jax.shard_map(
        shards, mesh=fine, in_specs=in_specs, out_specs=out_specs, check_vma=False
    )
```

```python
import functools

import jax
import jax.numpy as jnp
from jax import lax
from jax.experimental import pallas as pl
from jax.experimental.pallas import tpu as pltpu
from jax.sharding import Mesh, PartitionSpec as P

F32, BF16 = jnp.float32, jnp.bfloat16
HEADS, WIDTH, CHANNELS = 4, 32, 128
COLS, BLOCK, ROWS = 512, 512, 4
KEYS = 4 * BLOCK
SHARE = COLS // 16
PAD = 48
STEP = 2
LOG2E = 1.4426950408889634
LOW, HIGH = 1e-26, 1e30
ROW_AXES = ("y", "xh", "core")
COL_AXES = ("z", "xl")
VMEM_LIMIT = 40 * 2**20


def matmul(a, b, first=1, second=0):
    dims = (((first,), (second,)), ((), ()))
    return lax.dot_general(a, b, dims, preferred_element_type=F32)


def prepare_kernel(pair, gain, bias, normed, bias_t):
    keys = bias.shape[2]
    places = [lax.broadcasted_iota(jnp.int32, (keys, keys), axis) for axis in (0, 1)]
    identity = (places[0] == places[1]).astype(F32).astype(BF16)
    values = pair[...].astype(F32)
    centered = values - jnp.mean(values, axis=-1, keepdims=True)
    variance = jnp.mean(centered * centered, axis=-1, keepdims=True)
    normed[...] = (centered * lax.rsqrt(variance + 1e-05) * gain[...]).astype(BF16)
    for h in range(bias.shape[0]):
        bias_t[h] = matmul(identity, bias[h], 1, 1).astype(BF16)


def prepare(pair_block, norm_gain, head_bias):
    def whole(*shape):
        return pl.BlockSpec((2,) + shape, lambda i: (i, 0, 0))

    keys = head_bias.shape[2]
    return pl.pallas_call(
        prepare_kernel,
        grid=(ROWS // 2,),
        in_specs=[
            whole(COLS, CHANNELS),
            pl.BlockSpec((1, CHANNELS), lambda i: (0, 0)),
            whole(COLS, keys),
        ],
        out_specs=[whole(COLS, CHANNELS), whole(keys, COLS)],
        out_shape=[
            jax.ShapeDtypeStruct((ROWS, COLS, CHANNELS), BF16),
            jax.ShapeDtypeStruct((HEADS, keys, COLS), BF16),
        ],
        name="prepare",
    )(pair_block, norm_gain.reshape(1, CHANNELS), head_bias)


def attend_kernel(blocks, xq, *rest):
    xks, w, rest = rest[:blocks], rest[blocks], rest[blocks + 1 :]
    biases, out, scratch = rest[:10], rest[-10], rest[-9:]
    bias_s, scaled_s, top_s, k_s, v_s, q_s, gate_s, stat_s, sems = scratch
    step = pl.program_id(0)

    y, z, core = lax.axis_index("y"), lax.axis_index("z"), lax.axis_index("core")

    def bias_copies():
        copies = []
        for n, ref in enumerate(biases):
            place = (0, 1, 3, 2, 2)[n // 2]
            heads = pl.ds((0, 0, 0, 0, 2)[n // 2], ref.shape[0])
            slot = lax.rem(y - z + 4 + place, 4)
            half = core if n % 2 == 0 else 1 - core
            at = pl.ds(pl.multiple_of(half * 256, 256), 256)
            copies.append(pltpu.make_async_copy(ref, bias_s.at[slot, heads, at, :], sems.at[n]))
        return copies

    @pl.when(step == 0)
    def _():
        for copy in bias_copies():
            copy.start()
        q_s[...] = jnp.zeros_like(q_s)
        stat_s[...] = jnp.zeros_like(stat_s)
        v_s[:, :, WIDTH:, :] = jnp.ones((STEP, HEADS, PAD - WIDTH, KEYS), BF16)

    def project(r):
        x_q = xq[r]
        q_t = (matmul(w[:, :128], x_q, 0, 1) * WIDTH ** (-0.5)).astype(BF16)
        gate_s[r] = jax.nn.sigmoid(matmul(w[:, 384:], x_q, 0, 1))
        for h in range(HEADS):
            at = slice(h * WIDTH, (h + 1) * WIDTH)
            q_s[r, h, at, :] = q_t[at]
        start = 0
        for x in xks:
            size = x.shape[1]
            at = slice(start, start + size)
            k_s[r, at, :] = matmul(x[r], w[:, 128:256]).astype(BF16)
            v_t = matmul(w[:, 256:384], x[r], 0, 1).astype(BF16)
            for h in range(HEADS):
                v_s[r, h, :WIDTH, at] = v_t[h * WIDTH : (h + 1) * WIDTH]
            start += size

    def finish(r, totals, shifts):
        parts, stats = [], []
        for total, shift in zip(totals, shifts):
            mass = total[WIDTH : WIDTH + 1]
            parts.append(total[:WIDTH] * (1.0 / mass))
            stats.append(shift + jnp.log(mass))
        gated = jnp.concatenate(parts, axis=0) * gate_s[r]
        at = step * STEP + r
        out[:, at] = gated.T.astype(BF16).reshape(16, SHARE, CHANNELS)
        stat = jnp.concatenate(stats, axis=0)
        high = stat.astype(BF16).astype(F32)
        middle = (stat - high).astype(BF16).astype(F32)
        low = stat - high - middle
        rows = jnp.concatenate([high, middle, low, jnp.zeros_like(low)], axis=0)
        stat_s[pl.ds(pl.multiple_of(at * 32, 32), 16), :] = rows

    for r in range(STEP):
        project(r)

    @pl.when(step == 0)
    def _():
        for copy in bias_copies():
            copy.wait()
        for h in range(HEADS):
            tops = [jnp.max(bias_s[t, h], axis=0, keepdims=True) for t in range(4)]
            top = jnp.maximum(jnp.maximum(tops[0], tops[1]), jnp.maximum(tops[2], tops[3]))
            top = top.astype(F32)
            top_s[h : h + 1, :] = top
            for t in range(4):
                scaled_s[t, h] = (bias_s[t, h].astype(F32) - top) * LOG2E

    units = [(r, h, t) for r in range(STEP) for h in range(HEADS) for t in range(4)]

    def scores(r, h, t):
        at = slice(t * BLOCK, (t + 1) * BLOCK)
        return matmul(k_s[r, at, :], q_s[r, h])

    fine, totals = [], []
    ahead, total = scores(*units[0]), None
    for n, (r, h, t) in enumerate(units):
        s = ahead
        if n + 1 < len(units):
            ahead = scores(*units[n + 1])
        p = jnp.exp2(s * LOG2E + scaled_s[t, h]).astype(BF16)
        pv = matmul(v_s[r, h, :, t * BLOCK : (t + 1) * BLOCK], p)
        total = pv if t == 0 else total + pv
        if t < 3:
            continue
        totals.append(total)
        if h < HEADS - 1:
            continue
        finish(r, totals, [top_s[g : g + 1, :] for g in range(HEADS)])
        mass = jnp.concatenate([total[WIDTH : WIDTH + 1] for total in totals], axis=0)
        inside = jnp.logical_and(mass > LOW, mass < HIGH)
        fine.append(jnp.min(inside.astype(F32)) > 0.5)
        totals = []

    for r in range(STEP):

        @pl.when(jnp.logical_not(fine[r]))
        def _():
            totals, shifts = [], []
            for h in range(HEADS):

                def tile(t, carry):
                    largest, total = carry
                    at = pl.ds(pl.multiple_of(t * BLOCK, BLOCK), BLOCK)
                    s = matmul(k_s[r, at, :], q_s[r, h]) + bias_s[t, h].astype(F32)
                    fresh = jnp.maximum(largest, jnp.max(s, axis=0, keepdims=True))
                    p = jnp.exp2((s - fresh) * LOG2E).astype(BF16)
                    scale = jnp.exp2((largest - fresh) * LOG2E)
                    return fresh, total * scale + matmul(v_s[r, h, :, at], p)

                begin = jnp.full((1, COLS), -jnp.inf, F32), jnp.zeros((PAD, COLS), F32)
                largest, total = lax.fori_loop(0, 4, tile, begin)
                totals.append(total)
                shifts.append(largest)
            finish(r, totals, shifts)

    @pl.when(step == pl.num_programs(0) - 1)
    def _():
        out[:, ROWS] = stat_s[...].T.astype(BF16).reshape(16, SHARE, CHANNELS)


def attend(x_q, x_ks, w_project, biases, message=()):
    half = len(message)

    def rows(x):
        return pl.BlockSpec((STEP,) + x.shape[1:], lambda i: (i, 0, 0))

    scores = ROWS * HEADS * COLS * KEYS
    block = (16, ROWS + 1, SHARE, CHANNELS)
    return pl.pallas_call(
        functools.partial(attend_kernel, len(x_ks)),
        grid=(ROWS // STEP,),
        in_specs=[rows(x_q)]
        + [rows(x) for x in x_ks]
        + [pl.BlockSpec((CHANNELS, 512), lambda i: (0, 0))]
        + [pl.BlockSpec(memory_space=pl.ANY)] * (len(biases) + len(message)),
        out_specs=pl.BlockSpec(block, lambda i: (0, half, 0, 0)),
        out_shape=jax.ShapeDtypeStruct((16, 2 * (ROWS + 1), SHARE, CHANNELS), BF16),
        input_output_aliases={2 + len(x_ks) + len(biases): 0} if half else {},
        scratch_shapes=[
            pltpu.VMEM((4, HEADS, BLOCK, COLS), BF16),
            pltpu.VMEM((4, HEADS, BLOCK, COLS), F32),
            pltpu.VMEM((HEADS, COLS), F32),
            pltpu.VMEM((STEP, KEYS, CHANNELS), BF16),
            pltpu.VMEM((STEP, HEADS, PAD, KEYS), BF16),
            pltpu.VMEM((STEP, HEADS, CHANNELS, COLS), BF16),
            pltpu.VMEM((STEP, CHANNELS, COLS), F32),
            pltpu.VMEM((CHANNELS, COLS), F32),
            pltpu.SemaphoreType.DMA((10,)),
        ],
        compiler_params=pltpu.CompilerParams(vmem_limit_bytes=VMEM_LIMIT),
        cost_estimate=pl.CostEstimate(
            flops=scores * 512, bytes_accessed=2**24, transcendentals=scores
        ),
        name="attend",
    )(x_q, *x_ks, w_project, *biases, *message)


def merge_kernel(message, w, out):
    lane = lax.broadcasted_iota(jnp.int32, (CHANNELS, CHANNELS), 0)
    head = lax.broadcasted_iota(jnp.int32, (CHANNELS, CHANNELS), 1) // WIDTH
    rows = []
    for s in range(4):
        other = s ^ 2
        stat1, stat2 = message[s, ROWS], message[other, 2 * ROWS + 1]
        for i in range(ROWS):
            part = lane - 32 * i
            inside = (part >= 0) & (part < 12) & (lax.rem(part, 4) == head)
            pick = inside.astype(F32).astype(BF16)
            share = jax.nn.sigmoid(matmul(stat1, pick) - matmul(stat2, pick))
            o1 = message[s, i].astype(F32)
            o2 = message[other, ROWS + 1 + i].astype(F32)
            rows.append((o2 + share * (o1 - o2)).astype(BF16))
    update = matmul(jnp.concatenate(rows, axis=0), w[...])
    update = jnp.swapaxes(update.reshape(4 * ROWS, SHARE, CHANNELS), 0, 1)
    out[...] = update.astype(BF16)


def merge(message, w_out):
    return pl.pallas_call(
        merge_kernel,
        grid=(4,),
        in_specs=[
            pl.BlockSpec((4,) + message.shape[1:], lambda y: (y, 0, 0, 0)),
            pl.BlockSpec((CHANNELS, CHANNELS), lambda y: (0, 0)),
        ],
        out_specs=pl.BlockSpec((SHARE, 4 * ROWS, CHANNELS), lambda y: (0, y, 0)),
        out_shape=jax.ShapeDtypeStruct((SHARE, 16 * ROWS, CHANNELS), BF16),
        compiler_params=pltpu.CompilerParams(vmem_limit_bytes=VMEM_LIMIT),
        name="merge",
    )(message, w_out)


def tied(x, *before):
    for array in before:
        x = x + 0 * array[(0,) * array.ndim]
    return x


def shift(x, axis, step):
    return lax.ppermute(x, axis, [(i, (i + step) % 4) for i in range(4)])


def swap(x):
    return lax.ppermute(x, "core", [(0, 1), (1, 0)])


def gather_direct(x, axis):
    return x, shift(x, axis, -1), shift(x, axis, 2), shift(x, axis, 1)


def gather_ring(x, axis):
    behind, ahead = shift(x, axis, 1), shift(x, axis, -1)
    parts = tied(behind[:, :256], ahead), tied(ahead[:, 256:], behind)
    far = shift(parts[0], axis, 1), shift(parts[1], axis, -1)
    return x, ahead, *far, behind


def gather_bias(block):
    behind, ahead = shift(block, "y", 1), shift(block, "y", -1)
    far = [shift(behind[:2], "y", 1), shift(ahead[2:], "y", -1)]
    return [side for b in (block, ahead, behind, *far) for side in (b, swap(b))]


def shards(pair_block, norm_gain, w_project, w_out, head_bias):
    own, bias_t = prepare(pair_block, norm_gain, head_bias)
    biases = gather_bias(bias_t)

    xh, xl = lax.axis_index("xh"), lax.axis_index("xl")
    behind, ahead = shift(own, ("xh", "xl"), 1), shift(own, ("xh", "xl"), -1)
    opposite = shift(behind, ("xh", "xl"), 1)
    near = jnp.where(xh == 0, behind, ahead)
    first_ks = gather_ring(tied(jnp.where(xl == xh, own, near), biases[1]), "z")
    near = jnp.where(xh == 0, ahead, behind)
    second_ks = gather_direct(tied(jnp.where(xl == xh, opposite, near), first_ks[1], first_ks[4]), "z")

    message = attend(own, first_ks, w_project, biases)
    message = attend(opposite, second_ks, w_project, biases, (message,))
    message = lax.all_to_all(message, ROW_AXES, split_axis=0, concat_axis=0, tiled=True)
    return merge(message, w_out)


def solution(mesh):
    fine = Mesh(mesh.devices.reshape(4, 2, 2, 4, 2), ROW_AXES + COL_AXES)
    in_specs = (P(ROW_AXES, COL_AXES, None), P(), P(), P(), P(None, COL_AXES, ROW_AXES))
    out_specs = P(COL_AXES + ROW_AXES, None, None)
    return jax.shard_map(
        shards, mesh=fine, in_specs=in_specs, out_specs=out_specs, check_vma=False
    )
```

```python
import functools

import jax
import jax.numpy as jnp
from jax import lax
from jax.experimental import pallas as pl
from jax.experimental.pallas import tpu as pltpu
from jax.sharding import Mesh, PartitionSpec as P

F32, BF16 = jnp.float32, jnp.bfloat16
HEADS, WIDTH, CHANNELS = 4, 32, 128
COLS, BLOCK, ROWS = 512, 512, 4
KEYS = 4 * BLOCK
SHARE = COLS // 16
PAD = 48
STEP = 2
LOG2E = 1.4426950408889634
LOW, HIGH = 1e-26, 1e30
ROW_AXES = ("y", "xh", "core")
COL_AXES = ("z", "xl")
VMEM_LIMIT = 40 * 2**20


def matmul(a, b, first=1, second=0):
    dims = (((first,), (second,)), ((), ()))
    return lax.dot_general(a, b, dims, preferred_element_type=F32)


def prepare_kernel(pair, gain, bias, normed, bias_t):
    keys = bias.shape[2]
    places = [lax.broadcasted_iota(jnp.int32, (keys, keys), axis) for axis in (0, 1)]
    identity = (places[0] == places[1]).astype(F32).astype(BF16)
    values = pair[...].astype(F32)
    centered = values - jnp.mean(values, axis=-1, keepdims=True)
    variance = jnp.mean(centered * centered, axis=-1, keepdims=True)
    normed[...] = (centered * lax.rsqrt(variance + 1e-05) * gain[...]).astype(BF16)
    for h in range(bias.shape[0]):
        bias_t[h] = matmul(identity, bias[h], 1, 1).astype(BF16)


def prepare(pair_block, norm_gain, head_bias):
    def whole(*shape):
        return pl.BlockSpec((ROWS,) + shape, lambda i: (i, 0, 0))

    keys = head_bias.shape[2]
    return pl.pallas_call(
        prepare_kernel,
        grid=(1,),
        in_specs=[
            whole(COLS, CHANNELS),
            pl.BlockSpec((1, CHANNELS), lambda i: (0, 0)),
            whole(COLS, keys),
        ],
        out_specs=[whole(COLS, CHANNELS), whole(keys, COLS)],
        out_shape=[
            jax.ShapeDtypeStruct((ROWS, COLS, CHANNELS), BF16),
            jax.ShapeDtypeStruct((HEADS, keys, COLS), BF16),
        ],
        name="prepare",
    )(pair_block, norm_gain.reshape(1, CHANNELS), head_bias)


def attend_kernel(blocks, xq, *rest):
    xks, w, rest = rest[:blocks], rest[blocks], rest[blocks + 1 :]
    biases, out, scratch = rest[:10], rest[-10], rest[-9:]
    bias_s, scaled_s, top_s, k_s, v_s, q_s, gate_s, stat_s, sems = scratch
    step = pl.program_id(0)

    y, z, core = lax.axis_index("y"), lax.axis_index("z"), lax.axis_index("core")

    def bias_copies():
        copies = []
        for n, ref in enumerate(biases):
            place = (0, 1, 3, 2, 2)[n // 2]
            heads = pl.ds((0, 0, 0, 0, 2)[n // 2], ref.shape[0])
            slot = lax.rem(y - z + 4 + place, 4)
            half = core if n % 2 == 0 else 1 - core
            at = pl.ds(pl.multiple_of(half * 256, 256), 256)
            copies.append(pltpu.make_async_copy(ref, bias_s.at[slot, heads, at, :], sems.at[n]))
        return copies

    @pl.when(step == 0)
    def _():
        for copy in bias_copies():
            copy.start()
        q_s[...] = jnp.zeros_like(q_s)
        stat_s[...] = jnp.zeros_like(stat_s)
        v_s[:, :, WIDTH:, :] = jnp.ones((STEP, HEADS, PAD - WIDTH, KEYS), BF16)

    def project(r):
        x_q = xq[r]
        q_t = (matmul(w[:, :128], x_q, 0, 1) * WIDTH ** (-0.5)).astype(BF16)
        gate_s[r] = jax.nn.sigmoid(matmul(w[:, 384:], x_q, 0, 1))
        for h in range(HEADS):
            at = slice(h * WIDTH, (h + 1) * WIDTH)
            q_s[r, h, at, :] = q_t[at]
        start = 0
        for x in xks:
            size = x.shape[1]
            at = slice(start, start + size)
            k_s[r, at, :] = matmul(x[r], w[:, 128:256]).astype(BF16)
            v_t = matmul(w[:, 256:384], x[r], 0, 1).astype(BF16)
            for h in range(HEADS):
                v_s[r, h, :WIDTH, at] = v_t[h * WIDTH : (h + 1) * WIDTH]
            start += size

    def finish(r, totals, shifts):
        parts, stats = [], []
        for total, shift in zip(totals, shifts):
            mass = total[WIDTH : WIDTH + 1]
            parts.append(total[:WIDTH] * (1.0 / mass))
            stats.append(shift + jnp.log(mass))
        gated = jnp.concatenate(parts, axis=0) * gate_s[r]
        at = step * STEP + r
        out[:, at] = gated.T.astype(BF16).reshape(16, SHARE, CHANNELS)
        stat = jnp.concatenate(stats, axis=0)
        high = stat.astype(BF16).astype(F32)
        middle = (stat - high).astype(BF16).astype(F32)
        low = stat - high - middle
        rows = jnp.concatenate([high, middle, low, jnp.zeros_like(low)], axis=0)
        stat_s[pl.ds(pl.multiple_of(at * 32, 32), 16), :] = rows

    for r in range(STEP):
        project(r)

    @pl.when(step == 0)
    def _():
        for copy in bias_copies():
            copy.wait()
        for h in range(HEADS):
            tops = [jnp.max(bias_s[t, h], axis=0, keepdims=True) for t in range(4)]
            top = jnp.maximum(jnp.maximum(tops[0], tops[1]), jnp.maximum(tops[2], tops[3]))
            top = top.astype(F32)
            top_s[h : h + 1, :] = top
            for t in range(4):
                scaled_s[t, h] = (bias_s[t, h].astype(F32) - top) * LOG2E

    units = [(r, h, t) for r in range(STEP) for h in range(HEADS) for t in range(4)]

    def scores(r, h, t):
        at = slice(t * BLOCK, (t + 1) * BLOCK)
        return matmul(k_s[r, at, :], q_s[r, h])

    fine, totals = [], []
    ahead, total = scores(*units[0]), None
    for n, (r, h, t) in enumerate(units):
        s = ahead
        if n + 1 < len(units):
            ahead = scores(*units[n + 1])
        p = jnp.exp2(s * LOG2E + scaled_s[t, h]).astype(BF16)
        pv = matmul(v_s[r, h, :, t * BLOCK : (t + 1) * BLOCK], p)
        total = pv if t == 0 else total + pv
        if t < 3:
            continue
        totals.append(total)
        if h < HEADS - 1:
            continue
        finish(r, totals, [top_s[g : g + 1, :] for g in range(HEADS)])
        mass = jnp.concatenate([total[WIDTH : WIDTH + 1] for total in totals], axis=0)
        inside = jnp.logical_and(mass > LOW, mass < HIGH)
        fine.append(jnp.min(inside.astype(F32)) > 0.5)
        totals = []

    for r in range(STEP):

        @pl.when(jnp.logical_not(fine[r]))
        def _():
            totals, shifts = [], []
            for h in range(HEADS):

                def tile(t, carry):
                    largest, total = carry
                    at = pl.ds(pl.multiple_of(t * BLOCK, BLOCK), BLOCK)
                    s = matmul(k_s[r, at, :], q_s[r, h]) + bias_s[t, h].astype(F32)
                    fresh = jnp.maximum(largest, jnp.max(s, axis=0, keepdims=True))
                    p = jnp.exp2((s - fresh) * LOG2E).astype(BF16)
                    scale = jnp.exp2((largest - fresh) * LOG2E)
                    return fresh, total * scale + matmul(v_s[r, h, :, at], p)

                begin = jnp.full((1, COLS), -jnp.inf, F32), jnp.zeros((PAD, COLS), F32)
                largest, total = lax.fori_loop(0, 4, tile, begin)
                totals.append(total)
                shifts.append(largest)
            finish(r, totals, shifts)

    @pl.when(step == pl.num_programs(0) - 1)
    def _():
        out[:, ROWS] = stat_s[...].T.astype(BF16).reshape(16, SHARE, CHANNELS)


def attend(x_q, x_ks, w_project, biases, message=()):
    half = len(message)

    def rows(x):
        return pl.BlockSpec((STEP,) + x.shape[1:], lambda i: (i, 0, 0))

    scores = ROWS * HEADS * COLS * KEYS
    block = (16, ROWS + 1, SHARE, CHANNELS)
    return pl.pallas_call(
        functools.partial(attend_kernel, len(x_ks)),
        grid=(ROWS // STEP,),
        in_specs=[rows(x_q)]
        + [rows(x) for x in x_ks]
        + [pl.BlockSpec((CHANNELS, 512), lambda i: (0, 0))]
        + [pl.BlockSpec(memory_space=pl.ANY)] * (len(biases) + len(message)),
        out_specs=pl.BlockSpec(block, lambda i: (0, half, 0, 0)),
        out_shape=jax.ShapeDtypeStruct((16, 2 * (ROWS + 1), SHARE, CHANNELS), BF16),
        input_output_aliases={2 + len(x_ks) + len(biases): 0} if half else {},
        scratch_shapes=[
            pltpu.VMEM((4, HEADS, BLOCK, COLS), BF16),
            pltpu.VMEM((4, HEADS, BLOCK, COLS), F32),
            pltpu.VMEM((HEADS, COLS), F32),
            pltpu.VMEM((STEP, KEYS, CHANNELS), BF16),
            pltpu.VMEM((STEP, HEADS, PAD, KEYS), BF16),
            pltpu.VMEM((STEP, HEADS, CHANNELS, COLS), BF16),
            pltpu.VMEM((STEP, CHANNELS, COLS), F32),
            pltpu.VMEM((CHANNELS, COLS), F32),
            pltpu.SemaphoreType.DMA((10,)),
        ],
        compiler_params=pltpu.CompilerParams(vmem_limit_bytes=VMEM_LIMIT),
        cost_estimate=pl.CostEstimate(
            flops=scores * 512, bytes_accessed=2**24, transcendentals=scores
        ),
        name="attend",
    )(x_q, *x_ks, w_project, *biases, *message)


def merge_kernel(message, w, out):
    lane = lax.broadcasted_iota(jnp.int32, (CHANNELS, CHANNELS), 0)
    head = lax.broadcasted_iota(jnp.int32, (CHANNELS, CHANNELS), 1) // WIDTH
    rows = []
    for s in range(4):
        other = s ^ 2
        stat1, stat2 = message[s, ROWS], message[other, 2 * ROWS + 1]
        for i in range(ROWS):
            part = lane - 32 * i
            inside = (part >= 0) & (part < 12) & (lax.rem(part, 4) == head)
            pick = inside.astype(F32).astype(BF16)
            share = jax.nn.sigmoid(matmul(stat1, pick) - matmul(stat2, pick))
            o1 = message[s, i].astype(F32)
            o2 = message[other, ROWS + 1 + i].astype(F32)
            rows.append((o2 + share * (o1 - o2)).astype(BF16))
    update = matmul(jnp.concatenate(rows, axis=0), w[...])
    update = jnp.swapaxes(update.reshape(4 * ROWS, SHARE, CHANNELS), 0, 1)
    out[...] = update.astype(BF16)


def merge(message, w_out):
    return pl.pallas_call(
        merge_kernel,
        grid=(4,),
        in_specs=[
            pl.BlockSpec((4,) + message.shape[1:], lambda y: (y, 0, 0, 0)),
            pl.BlockSpec((CHANNELS, CHANNELS), lambda y: (0, 0)),
        ],
        out_specs=pl.BlockSpec((SHARE, 4 * ROWS, CHANNELS), lambda y: (0, y, 0)),
        out_shape=jax.ShapeDtypeStruct((SHARE, 16 * ROWS, CHANNELS), BF16),
        compiler_params=pltpu.CompilerParams(vmem_limit_bytes=VMEM_LIMIT),
        name="merge",
    )(message, w_out)


def tied(x, *before):
    for array in before:
        x = x + 0 * array[(0,) * array.ndim]
    return x


def shift(x, axis, step):
    return lax.ppermute(x, axis, [(i, (i + step) % 4) for i in range(4)])


def swap(x):
    return lax.ppermute(x, "core", [(0, 1), (1, 0)])


def gather_direct(x, axis):
    return x, shift(x, axis, -1), shift(x, axis, 2), shift(x, axis, 1)


def gather_ring(x, axis):
    behind, ahead = shift(x, axis, 1), shift(x, axis, -1)
    parts = tied(behind[:, :256], ahead), tied(ahead[:, 256:], behind)
    far = shift(parts[0], axis, 1), shift(parts[1], axis, -1)
    return x, ahead, *far, behind


def gather_bias(block):
    behind, ahead = shift(block, "y", 1), shift(block, "y", -1)
    far = [shift(behind[:2], "y", 1), shift(ahead[2:], "y", -1)]
    return [side for b in (block, ahead, behind, *far) for side in (b, swap(b))]


def shards(pair_block, norm_gain, w_project, w_out, head_bias):
    own, bias_t = prepare(pair_block, norm_gain, head_bias)
    biases = gather_bias(bias_t)

    xh, xl = lax.axis_index("xh"), lax.axis_index("xl")
    behind, ahead = shift(own, ("xh", "xl"), 1), shift(own, ("xh", "xl"), -1)
    opposite = shift(behind, ("xh", "xl"), 1)
    near = jnp.where(xh == 0, behind, ahead)
    first_ks = gather_ring(tied(jnp.where(xl == xh, own, near), biases[1]), "z")
    near = jnp.where(xh == 0, ahead, behind)
    second_ks = gather_direct(tied(jnp.where(xl == xh, opposite, near), first_ks[1], first_ks[4]), "z")

    message = attend(own, first_ks, w_project, biases)
    message = attend(opposite, second_ks, w_project, biases, (message,))
    message = lax.all_to_all(message, ROW_AXES, split_axis=0, concat_axis=0, tiled=True)
    return merge(message, w_out)


def solution(mesh):
    fine = Mesh(mesh.devices.reshape(4, 2, 2, 4, 2), ROW_AXES + COL_AXES)
    in_specs = (P(ROW_AXES, COL_AXES, None), P(), P(), P(), P(None, COL_AXES, ROW_AXES))
    out_specs = P(COL_AXES + ROW_AXES, None, None)
    return jax.shard_map(
        shards, mesh=fine, in_specs=in_specs, out_specs=out_specs, check_vma=False
    )
```
